128 devices in a mesh: pairs: 4 (over z), virt: 32 (over x, y, core).
Axes of the slice: x: 4, y: 4, z: 4, core: 2. Of those that a mesh axis runs over, the one named last changes fastest.
Arguments:
- amps: bfloat16 [32, 512, 64, 256], P('virt', 'pairs'), may hold values from -6 to 6
- fock: bfloat16 [2048, 2048], P(('pairs', 'virt')), may hold values from -0.375 to 0.375
- cols: int32 [32, 512, 4], P(None, 'pairs'), may hold values from 0 to 31, all different within a row; in each aligned block of 128 rows (0 to 127, 128 to 255, ..., all dimensions but the last counted through in order) at most 32 rows name the same one
Outputs:
- residual: float32 [32, 512, 64, 256], P('virt', 'pairs')
The draws below stay inside these ranges and needn't reach their ends.
Inputs may be any that keep to these rules, and one draw needn't show every extreme that they name: `cols`: within one row tile and one aligned block of 128 pair rows, no column tile is named by more than 32 rows, and some column tile is named by exactly 32; the 4 numbers of one row differ.
All inputs are finite; a program needn't handle non-finite values.
Results may differ from the reference program's by a relative error of at most 0.0021.
Values may be sent and summed in bfloat16 or wider, within the bound.
A program may use at most 256 MiB of HBM per device.

```python
import math
import jax
import jax.numpy as jnp
import numpy as np
from jax import lax

TILE = 64
NT = 32
KEPT = 4
PR = 128
NV = 2048
P_SIZE = 512
MOST = 32


def steps_of(own_key, extent, pieces, least, largest):
    level, own = 1.0, jax.random.fold_in(own_key, 6)
    for axis_at, blocks in pieces:
        heights = jnp.exp(jax.random.uniform(jax.random.fold_in(own, axis_at), (blocks,), jnp.float32, least / len(pieces), largest / len(pieces)))
        level = level * jnp.repeat(heights, extent[axis_at] // blocks).reshape([-1 if axis == axis_at else 1 for axis in range(len(extent))])
    return level


def assign_block(own_key, own, number, rows, count, top, reach, skew):
    ranking = jax.random.permutation(own_key, count)
    heavy_load, ordinary = load_shares(count, rows * top, reach, skew, True), load_shares(count, rows * top, reach, skew, False)
    places = jnp.arange(count)

    def named(tallies, rotation):
        used = int((tallies > 0).sum())
        fixed = max(1, used // 4)
        moved = fixed + (places - fixed + rotation * (used - fixed)) % max(1, count - fixed)
        return jnp.zeros((count,), jnp.int32).at[ranking[jnp.where(places < fixed, places, moved)]].set(jnp.asarray(tallies, jnp.int32))

    tallies = jnp.where(number % 4 == 0, named(heavy_load, number // 4), named(ordinary, number - number // 4 - 1))
    mixed = jax.random.permutation(jax.random.fold_in(own, 3), count)
    donor, receiver = mixed[0:count // 2 * 2:2], mixed[1:count // 2 * 2:2]
    room = jnp.minimum(tallies[donor] - 1, reach - tallies[receiver]) // 2
    room = jnp.where((donor == ranking[0]) | (receiver == ranking[0]) | (tallies[receiver] == 0), 0, jnp.maximum(room, 0))
    moved = jax.random.randint(jax.random.fold_in(own, 4), (count // 2,), 0, 1 << 20) % (room + 1)
    tallies = tallies.at[donor].add(-moved).at[receiver].add(moved)
    members = jnp.searchsorted(jnp.cumsum(tallies), jnp.arange(rows * top), side="right").astype(jnp.int32)
    table = members.reshape(top, rows).T
    table = table[jax.random.permutation(jax.random.fold_in(own, 1), rows)]
    rotation = jax.random.randint(jax.random.fold_in(own, 2), (rows, 1), 0, top)
    return jnp.take_along_axis(table, (jnp.arange(top)[None, :] + rotation) % top, axis=1)


def load_shares(number_of, total, bound, lean, full):
    weights = [(1 << 20) // math.isqrt(standing ** lean) + 1 for standing in range(1, number_of + 1)]
    largest = bound if full else min(bound, max(-(-total // number_of), total * weights[0] // sum(weights)))
    least = 1 if total - largest >= number_of - 1 else 0
    counts, spare = [largest] + [least] * (number_of - 1), total - largest - least * (number_of - 1)
    while spare > 0:
        movable = [i for i in range(1, number_of) if counts[i] < largest] or [i for i in range(1, number_of) if counts[i] < bound]
        pool, remaining = sum([weights[i] for i in movable]), spare
        for i in movable:
            more = min(bound - counts[i], max(1, remaining * weights[i] // pool), spare)
            counts[i] = counts[i] + more
            spare = spare - more
    return np.array(counts)


def gaussian(own_key, shape, scale, limit, cuts=(), kind=jnp.bfloat16):
    drawn = jax.random.normal(own_key, shape, jnp.float32) * scale
    if len(cuts) > 0:
        drawn = steps_of(own_key, shape, cuts, -0.22, 0.18) * drawn
    return jnp.clip(drawn, min=-limit, max=limit).astype(kind)


def setup_inputs(seed: int = 0) -> dict:
    seeds = jax.random.split(jax.random.key(seed), 4)
    amps = gaussian(seeds[0], (NT, P_SIZE, TILE, KEPT * TILE), 1.0, 6.0, ((0, 32), (1, 4)))
    fock = gaussian(seeds[1], (NV, NV), (KEPT * TILE) ** -0.5, 0.375, ((0, 128),))
    cols_keys = jax.random.split(jax.random.fold_in(seeds[2], 1), NT * P_SIZE // PR)
    cols_turns = jax.random.permutation(jax.random.fold_in(seeds[2], 3), NT * P_SIZE // PR)
    cols = jax.vmap(lambda own, number: assign_block(jax.random.fold_in(seeds[2], 2), own, number, PR, NT, KEPT, MOST, 2))(cols_keys, cols_turns).reshape((NT, P_SIZE, KEPT))
    return {"amps": amps, "fock": fock, "cols": cols}


def dress_tiles(tile_rows, col_list, targets, fock_tiles):
    count = tile_rows.shape[0]
    chosen = fock_tiles[targets[:, :, None], :, col_list[:, None, :], :]
    split_rows = tile_rows.reshape(count, TILE, KEPT, TILE).astype(jnp.float32)
    return jnp.einsum('mxkc,mjkyc->mjxy', split_rows, chosen.astype(jnp.float32))


def reference(amps, fock, cols):
    fock_tiles = fock.reshape(NT, TILE, NT, TILE)
    pair_index = jnp.arange(P_SIZE, dtype=jnp.int32)
    mirror_row = (pair_index // PR) * PR + (PR - 1 - pair_index % PR)

    def per_tile(row_tile):
        tile_rows = amps[row_tile]
        col_list = cols[row_tile]
        own_part = dress_tiles(tile_rows, col_list, col_list, fock_tiles)
        mirror_rows = amps[col_list, mirror_row[:, None]]
        mirror_cols = cols[col_list, mirror_row[:, None]]
        targets = jnp.zeros((P_SIZE * KEPT, 1), jnp.int32) + row_tile.astype(jnp.int32)
        mirrored = dress_tiles(mirror_rows.reshape(P_SIZE * KEPT, TILE, KEPT * TILE), mirror_cols.reshape(P_SIZE * KEPT, KEPT), targets, fock_tiles)
        rounded = lax.optimization_barrier(mirrored.reshape(P_SIZE, KEPT, TILE, TILE).astype(jnp.bfloat16))
        combined = own_part + jnp.transpose(rounded.astype(jnp.float32), (0, 1, 3, 2))
        return jnp.transpose(combined, (0, 2, 1, 3)).reshape(P_SIZE, TILE, KEPT * TILE)

    return lax.map(per_tile, jnp.arange(NT, dtype=jnp.int32))
```

```python
import functools

import jax
import jax.numpy as jnp
from jax import lax
from jax.experimental import pallas as pl
from jax.experimental.pallas import tpu as pltpu
from jax.sharding import PartitionSpec as P

MESH = pl.DeviceIdType.MESH
TILE = 64
KEPT = 4
ROWS = 128
NTILES = 32
NSIDE = 4
SPLITS = 4
SLOTS = 32
PER = SLOTS // SPLITS
PARTS = ((0, 5, "zyx"), (5, 5, "xzy"), (10, 6, "yxz"))
LANES = 16


def place(pos):
    return (pos["z"], pos["x"] * 8 + pos["y"] * 2 + pos["c"])


def moved(pos, axis, by):
    new = dict(pos)
    new[axis] = lax.rem(pos[axis] + by + 4, 4)
    return new


def exchange_kernel(
    rows_ref, cols_ref, at_ref, fock_ref, amps_ref, own_hbm, recv_hbm,
    ff, send, own, gsend, grecv, csend, crecv, tsend, trecv, lsem,
):
    zi = lax.axis_index("pairs")
    vi = lax.axis_index("virt")
    pos = {"x": vi // 8, "y": lax.rem(vi // 2, 4), "z": zi, "c": lax.rem(vi, 2)}

    def peer(off):
        px = lax.rem(pos["x"] + off // 8, 4)
        py = lax.rem(pos["y"] + lax.rem(off // 2, 4), 4)
        pc = lax.rem(pos["c"] + lax.rem(off, 2), 2)
        return px * 8 + py * 2 + pc

    def home(where, full, lo, width):
        z, x = [slice(None) if axis in full else where[axis] for axis in "zx"]
        high, low_y = slice(None), slice(None)
        if "y" not in full:
            high, low_y = where["y"] // 2, lax.rem(where["y"], 2)
        return ff.at[pl.ds(lo, width), z, x, high, low_y, where["c"]]

    barrier = pltpu.get_barrier_semaphore()

    def greet(off, carry):
        pl.semaphore_signal(barrier, inc=1, device_id=(zi, peer(off)), device_id_type=MESH)
        return carry

    lax.fori_loop(1, NTILES, greet, 0)
    for by in (1, 2, 3):
        pl.semaphore_signal(
            barrier, inc=1, device_id=place(moved(pos, "z", by)), device_id_type=MESH
        )
    mine = pltpu.make_async_copy(fock_ref, home(pos, "", 0, LANES), lsem)
    mine.start()
    mine.wait()
    pl.semaphore_wait(barrier, NTILES - 1 + 3)

    def block(part, where, full):
        lo, width, _ = PARTS[part]
        return home(where, full, lo, width)

    def push(part, number, where, full, axis, by):
        target = moved(pos, axis, by)
        ref = block(part, where, full)
        copy = pltpu.make_async_remote_copy(
            src_ref=ref, dst_ref=ref, send_sem=gsend.at[part, number],
            recv_sem=grecv.at[part, number], device_id=place(target), device_id_type=MESH,
        )
        copy.start()
        sent.append(copy)

    def arrived(part, number, where, full):
        ref = block(part, where, full)
        pltpu.make_async_remote_copy(
            src_ref=ref, dst_ref=ref, send_sem=gsend.at[part, number],
            recv_sem=grecv.at[part, number], device_id=place(moved(pos, "z", 1)),
            device_id_type=MESH,
        ).wait_recv()

    twin = {**pos, "c": 1 - pos["c"]}

    def across(part, number, where, full):
        ref = block(part, where, full)
        copy = pltpu.make_async_remote_copy(
            src_ref=ref, dst_ref=ref, send_sem=csend.at[part, number],
            recv_sem=crecv.at[part, number], device_id=place(twin), device_id_type=MESH,
        )
        copy.start()
        sent.append(copy)

    def came_across(part, number, where, full):
        ref = block(part, {**where, "c": twin["c"]}, full)
        pltpu.make_async_remote_copy(
            src_ref=ref, dst_ref=ref, send_sem=csend.at[part, number],
            recv_sem=crecv.at[part, number], device_id=place(twin), device_id_type=MESH,
        ).wait_recv()

    sent = []
    every = range(len(PARTS))
    for part in every:
        first = PARTS[part][2][0]
        for by in (1, 2, 3):
            push(part, by - 1, pos, "", first, by)
    for part in every:
        first, second, third = PARTS[part][2]
        for by in (1, 2, 3):
            arrived(part, by - 1, moved(pos, first, -by), "")
        for by in (1, 2, 3):
            push(part, 2 + by, pos, first, second, by)
        for by in (1, 2, 3):
            push(part, 5 + by, pos, first, third, by)
        across(part, 0, pos, first)
    for back in (1, 2, 3):
        for part in every:
            first, second, third = PARTS[part][2]
            where = moved(pos, second, -back)
            arrived(part, 2 + back, where, first)
            for by in (1, 2, 3):
                push(part, 5 + 3 * back + by, where, first, third, by)
            across(part, back, where, first)
    for back in range(4):
        for part in every:
            first, second, third = PARTS[part][2]
            where = moved(pos, second, -back)
            for by in (1, 2, 3):
                there = moved(where, third, -by)
                arrived(part, 5 + 3 * back + by, there, first)
                across(part, 4 * by + back, there, first)
    for back in range(4):
        for part in every:
            first, second, third = PARTS[part][2]
            where = moved(pos, second, -back)
            for by in range(4):
                came_across(part, 4 * by + back, moved(where, third, -by), first)
    for copy in sent:
        copy.wait_send()

    def swap_halves(s, carry):
        at = (s // 8, lax.rem(s // 2, 4), lax.rem(s, 2))
        for t in range(LANES):
            got = ff[(t,) + at].reshape(TILE, 128)
            turned = jnp.concatenate([got[:, TILE:], got[:, :TILE]], axis=1)
            ff[(LANES + t,) + at] = turned.reshape(2, 2, 16, 128)
        return carry

    lax.fori_loop(0, NTILES, swap_halves, 0)

    low = lax.broadcasted_iota(jnp.int32, (TILE, 128), 1) < TILE

    def tile_row(tile, cols):
        got = [ff[(col,) + tile].reshape(TILE, 128) for col in cols]
        return jnp.concatenate(
            [jnp.where(low, got[0], got[1]), jnp.where(low, got[2], got[3])], axis=1
        )

    def dressed(tile, slot):
        row = rows_ref[tile * SLOTS + slot]
        cols = [cols_ref[row, k] for k in range(KEPT)]
        at = (tile // 8, lax.rem(tile // 2, 4), lax.rem(tile, 2))
        return lax.dot_general(
            tile_row(at, cols), amps_ref[row], (((1,), (1,)), ((), ())),
            preferred_element_type=jnp.float32,
        )

    def tile_copy(step, tile, split):
        return pltpu.make_async_remote_copy(
            src_ref=send.at[step], dst_ref=recv_hbm.at[vi, split], send_sem=tsend.at[step],
            recv_sem=trecv.at[step], device_id=(zi, tile), device_id_type=MESH,
        )

    def offset_of(step):
        return lax.rem(lax.rem(step, 32) * 13 + 13, 32)

    def mirror(step, carry):
        split = step // 32
        off = offset_of(step)
        tile = peer(off)
        for s in range(0, PER, 2):
            pair = [dressed(tile, split * PER + s + i).astype(jnp.bfloat16) for i in (0, 1)]
            send[step, s // 2] = jnp.concatenate(pair, axis=1)

        @pl.when(off != 0)
        def _():
            tile_copy(step, tile, split).start()

        @pl.when(off == 0)
        def _():
            pltpu.make_async_copy(
                send.at[step], recv_hbm.at[vi, split], tsend.at[step]
            ).start()

        return carry

    lax.fori_loop(0, NTILES * SPLITS, mirror, 0)

    def own_row(row, carry):
        cols = [cols_ref[row, k] for k in range(KEPT)]
        tiles = [tuple(at_ref[i, row, k] for i in range(3)) for k in range(KEPT)]
        weights = jnp.concatenate([tile_row(tile, cols) for tile in tiles], axis=0)
        own[row] = lax.dot_general(
            amps_ref[row], weights, (((1,), (1,)), ((), ())), preferred_element_type=jnp.float32
        )
        return carry

    lax.fori_loop(0, ROWS, own_row, 0)
    out_copy = pltpu.make_async_copy(own, own_hbm, lsem)
    out_copy.start()

    def finish(step, carry):
        split = step // 32
        off = offset_of(step)

        @pl.when(off != 0)
        def _():
            copy = tile_copy(step, peer(off), split)
            copy.wait_send()
            copy.wait_recv()

        @pl.when(off == 0)
        def _():
            pltpu.make_async_copy(
                send.at[step], recv_hbm.at[vi, split], tsend.at[step]
            ).wait()

        return carry

    lax.fori_loop(0, NTILES * SPLITS, finish, 0)
    out_copy.wait()


def combine_kernel(slot_ref, turn_ref, own_ref, recv_ref, out_ref):
    low = lax.broadcasted_iota(jnp.int32, (TILE, 128), 1) < TILE
    count = own_ref.shape[0]
    base = pl.program_id(0) * count
    for r in range(count):
        for h in range(2):
            halves = []
            for i in range(2):
                at = (base + r) * KEPT + 2 * h + i
                got = recv_ref[slot_ref[at]].astype(jnp.float32)
                halves.append(pltpu.roll(got, turn_ref[at], axis=1))
            out_ref[r, :, h * 128:(h + 1) * 128] = own_ref[r, :, h * 128:(h + 1) * 128] + jnp.where(
                low, halves[0], halves[1]
            )


def tables(cols, me):
    count = cols.shape[1]
    order = jnp.arange(count)
    named = jnp.any(cols == me, axis=2).astype(jnp.float32)
    upto = jnp.dot(named, (order[:, None] <= order[None, :]).astype(jnp.float32))
    slots = jnp.arange(SLOTS, dtype=jnp.float32)
    rank = jnp.sum((upto[:, None, :] <= slots[None, :, None]).astype(jnp.int32), axis=2)
    rows = count - 1 - jnp.minimum(rank, count - 1)
    my_cols = lax.dynamic_index_in_dim(cols, me, 0, keepdims=False)
    hot = (my_cols[:, :, None] == jnp.arange(NTILES, dtype=jnp.int32)).astype(jnp.float32)
    before = jnp.dot((order[:, None] > order[None, :]).astype(jnp.float32), jnp.sum(hot, axis=1))
    slot = jnp.sum(hot * before[:, None, :], axis=2).astype(jnp.int32)
    at = my_cols * (SLOTS // 2) + slot // 2
    turn = ((slot + jnp.arange(KEPT, dtype=jnp.int32)) % 2) * TILE
    version = (my_cols + jnp.arange(KEPT, dtype=jnp.int32)) % 2
    places = version * LANES + my_cols // 2
    parts = jnp.stack([my_cols // 8, my_cols // 2 % 4, my_cols % 2])
    return rows.reshape(-1), places, parts, at.reshape(-1), turn.reshape(-1)


def per_device(amps, fock, cols):
    me = lax.axis_index("virt")
    rows, places, parts, at, turn = tables(cols, me)
    vmem = pl.BlockSpec(memory_space=pltpu.VMEM)
    smem = pl.BlockSpec(memory_space=pltpu.SMEM)
    anywhere = pl.BlockSpec(memory_space=pl.ANY)
    own, received = pl.pallas_call(
        exchange_kernel,
        out_shape=(
            jax.ShapeDtypeStruct((ROWS, TILE, KEPT * TILE), jnp.float32),
            jax.ShapeDtypeStruct((NTILES, SPLITS, PER // 2, TILE, 2 * TILE), jnp.bfloat16),
        ),
        in_specs=[smem, smem, smem, anywhere, vmem],
        out_specs=(anywhere, anywhere),
        scratch_shapes=[
            pltpu.VMEM((2 * LANES, 4, 4, 2, 2, 2, 16, 128), jnp.bfloat16),
            pltpu.VMEM((NTILES * SPLITS, PER // 2, TILE, 2 * TILE), jnp.bfloat16),
            pltpu.VMEM((ROWS, TILE, KEPT * TILE), jnp.float32),
            pltpu.SemaphoreType.DMA((3, 18)),
            pltpu.SemaphoreType.DMA((3, 18)),
            pltpu.SemaphoreType.DMA((3, 16)),
            pltpu.SemaphoreType.DMA((3, 16)),
            pltpu.SemaphoreType.DMA((NTILES * SPLITS,)),
            pltpu.SemaphoreType.DMA((NTILES * SPLITS,)),
            pltpu.SemaphoreType.DMA,
        ],
        compiler_params=pltpu.CompilerParams(
            collective_id=0, has_side_effects=True, vmem_limit_bytes=50 * 2**20
        ),
    )(
        rows, places, parts, fock.reshape(16, LANES, 128).transpose(1, 0, 2),
        amps.reshape(ROWS, TILE, KEPT * TILE),
    )
    step = 8
    blocked = pl.BlockSpec((step, TILE, KEPT * TILE), lambda i: (i, 0, 0))
    out = pl.pallas_call(
        combine_kernel,
        grid=(ROWS // step,),
        out_shape=jax.ShapeDtypeStruct((ROWS, TILE, KEPT * TILE), jnp.float32),
        in_specs=[smem, smem, blocked, vmem],
        out_specs=blocked,
        compiler_params=pltpu.CompilerParams(vmem_limit_bytes=32 * 2**20),
    )(at, turn, own, received.reshape(NTILES * SLOTS // 2, TILE, 2 * TILE))
    return out[None]


def solution(mesh):
    in_specs = (P("virt", "pairs", None, None), P(("pairs", "virt"), None), P(None, "pairs", None))
    out_specs = P("virt", "pairs", None, None)
    return jax.shard_map(
        per_device, mesh=mesh, in_specs=in_specs, out_specs=out_specs, check_vma=False
    )
```

```python
import functools

import jax
import jax.numpy as jnp
from jax import lax
from jax.experimental import pallas as pl
from jax.experimental.pallas import tpu as pltpu
from jax.sharding import PartitionSpec as P

MESH = pl.DeviceIdType.MESH
TILE = 64
KEPT = 4
ROWS = 128
NTILES = 32
NSIDE = 4
SPLITS = 4
SLOTS = 32
PER = SLOTS // SPLITS
LANES = 16
CHUNK = 16
HALF = 1024


def place(pos):
    return (pos["z"], pos["x"] * 8 + pos["y"] * 2 + pos["c"])


def moved(pos, axis, by):
    new = dict(pos)
    new[axis] = lax.rem(pos[axis] + by + 4, 4)
    return new


def write_tables(me, cols_ref, vtab, vown, back_ref):
    f32, bf16, i32 = jnp.float32, jnp.bfloat16, jnp.int32
    mine = cols_ref[me]
    kept = lax.broadcasted_iota(i32, (KEPT, ROWS), 0)
    lane = lax.broadcasted_iota(i32, (KEPT, ROWS), 1)
    mine = jnp.minimum(jnp.maximum(mine, 0), NTILES - 1)
    spot = ((mine + kept) & 1) * LANES + (mine >> 1)
    vown[...] = jnp.concatenate([spot, mine], axis=0)
    first = lax.broadcasted_iota(i32, (ROWS, ROWS), 0)
    second = lax.broadcasted_iota(i32, (ROWS, ROWS), 1)
    upper = (first <= second).astype(f32).astype(bf16)
    flip = (first + second == ROWS - 1).astype(f32).astype(bf16)
    about = jnp.concatenate([spot, lane], axis=0).astype(f32).astype(bf16)
    about = jnp.dot(about, flip, preferred_element_type=f32).astype(bf16)
    named = jnp.sum((cols_ref[...] == me).astype(f32), axis=1)
    upto = jnp.dot(named.astype(bf16), upper, preferred_element_type=f32)
    rank = jnp.where(named > 0, upto, 0.0)
    slots = lax.broadcasted_iota(i32, (SLOTS, ROWS), 0).astype(f32) + 1.0
    entry = lax.broadcasted_iota(i32, (8, 8 * SLOTS), 0)
    largest = jnp.where(entry < KEPT, 2 * LANES - 1, ROWS - 1)
    for peer in range(0, NTILES, 8):
        hot = [
            (jnp.broadcast_to(rank[p:p + 1], (SLOTS, ROWS)) == slots).astype(f32).astype(bf16)
            for p in range(peer, peer + 8)
        ]
        got = lax.dot_general(
            about, jnp.concatenate(hot, axis=0), (((1,), (1,)), ((), ())),
            preferred_element_type=f32,
        )
        got = jnp.minimum(jnp.maximum(got.astype(i32), 0), largest)
        vtab[:, peer * SLOTS:(peer + 8) * SLOTS] = got
    number = lax.broadcasted_iota(i32, (NTILES, ROWS), 0)
    at = [jnp.broadcast_to(mine[k:k + 1], (NTILES, ROWS)) == number for k in range(KEPT)]
    count = sum(hit.astype(f32) for hit in at)
    before = jnp.dot(count.astype(bf16), upper, preferred_element_type=f32) - count
    slot = [jnp.sum(jnp.where(hit, before, 0.0), axis=0, keepdims=True) for hit in at]
    slot = jnp.minimum(jnp.maximum(jnp.concatenate(slot, axis=0).astype(i32), 0), SLOTS - 1)
    back_ref[...] = jnp.concatenate(
        [mine * (SLOTS // 2) + (slot >> 1), ((slot + kept) & 1) * TILE], axis=0
    )


def exchange_kernel(
    cols_ref, fock_ref, amps_hbm, own_hbm, recv_hbm, back_ref,
    land, fa, amps, send, own, vtab, vown, stab, sown,
    gsend, grecv, csend, crecv, tsend, trecv, lsem,
):
    zi = lax.axis_index("pairs")
    vi = lax.axis_index("virt")
    pos = {"x": vi // 8, "y": lax.rem(vi // 2, 4), "z": zi, "c": lax.rem(vi, 2)}
    twin = {**pos, "c": 1 - pos["c"]}

    load_amps = pltpu.make_async_copy(amps_hbm, amps, lsem.at[0])
    load_amps.start()

    barrier = pltpu.get_barrier_semaphore()

    def greet(off, carry):
        pl.semaphore_signal(
            barrier, inc=1, device_id=(zi, lax.rem(vi + off, NTILES)), device_id_type=MESH
        )
        return carry

    lax.fori_loop(1, NTILES, greet, 0)
    for by in (1, 2, 3):
        pl.semaphore_signal(
            barrier, inc=1, device_id=place(moved(pos, "z", by)), device_id_type=MESH
        )
    land[pos["z"], pos["x"], pos["y"], pos["c"]] = fock_ref[...]
    pl.semaphore_wait(barrier, NTILES - 1 + 3)

    sent = []

    def rows_at(where, full, half):
        at = [slice(None) if axis in full else where[axis] for axis in "zxy"]
        cols = slice(None) if half is None else pl.ds(half * HALF, HALF)
        return land.at[at[0], at[1], at[2], where["c"], :, cols]

    def copy_to(target, number, src, dst, out=gsend, into=grecv):
        return pltpu.make_async_remote_copy(
            src_ref=src, dst_ref=dst, send_sem=out.at[number], recv_sem=into.at[number],
            device_id=place(target), device_id_type=MESH,
        )

    def push(axis, by, number, where, full="", half=None, own_rows=False):
        dst = rows_at(where, full, half)
        src = dst
        if own_rows:
            src = fock_ref if half is None else fock_ref.at[:, pl.ds(half * HALF, HALF)]
        copy = copy_to(moved(pos, axis, by), number, src, dst)
        copy.start()
        sent.append(copy)

    def arrived(number, where, full="", half=None):
        ref = rows_at(where, full, half)
        copy_to(twin, number, ref, ref).wait_recv()

    def across(number, where, full="", half=None):
        ref = rows_at(where, full, half)
        copy = copy_to(twin, number, ref, ref, csend, crecv)
        copy.start()
        sent.append(copy)

    def came_across(number, where, full="", half=None):
        ref = rows_at({**where, "c": twin["c"]}, full, half)
        copy_to(twin, number, ref, ref, csend, crecv).wait_recv()

    def far(g):
        return moved(pos, "x", -g)

    def far_first(g):
        arrived(g - 1, far(g))
        for by in (1, 2, 3):
            push("y", by, 15 + 6 * (g - 1) + by - 1, far(g))

    def far_second(g):
        for by in (1, 2, 3):
            arrived(15 + 6 * (g - 1) + by - 1, moved(far(g), "y", -by))
        for by in (1, 2, 3):
            push("z", by, 18 + 6 * (g - 1) + by - 1, far(g), "y")
        across(8 + 4 * (g - 1), far(g), "y")

    def far_third(g):
        for by in (1, 2, 3):
            there = moved(far(g), "z", -by)
            arrived(18 + 6 * (g - 1) + by - 1, there, "y")
            across(8 + 4 * (g - 1) + by, there, "y")

    def far_last(g):
        for by in range(4):
            came_across(8 + 4 * (g - 1) + by, moved(far(g), "z", -by), "y")

    for by in (1, 2, 3):
        push("z", by, 3 + by - 1, pos, half=0, own_rows=True)
        push("y", by, 6 + by - 1, pos, half=1, own_rows=True)
    for by in (1, 2, 3):
        push("x", by, by - 1, pos, own_rows=True)
    write_tables(vi, cols_ref, vtab, vown, back_ref)
    job_table = pltpu.make_async_copy(vtab, stab, lsem.at[1])
    own_table = pltpu.make_async_copy(vown, sown, lsem.at[2])
    job_table.start()
    own_table.start()
    for half, axis, other in ((0, "z", "y"), (1, "y", "z")):
        for by in (1, 2, 3):
            arrived(3 + 3 * half + by - 1, moved(pos, axis, -by), half=half)
        for by in (1, 2, 3):
            push(other, by, 9 + 3 * half + by - 1, pos, axis, half)
        across(4 * half, pos, axis, half)
    for g in (1, 2, 3):
        far_first(g)
    for by in (1, 2, 3):
        for half, axis, other in ((0, "z", "y"), (1, "y", "z")):
            there = moved(pos, other, -by)
            arrived(9 + 3 * half + by - 1, there, axis, half)
            across(4 * half + by, there, axis, half)
    far_second(1)
    for by in range(4):
        for half, axis, other in ((0, "z", "y"), (1, "y", "z")):
            came_across(4 * half + by, moved(pos, other, -by), axis, half)
    job_table.wait()
    own_table.wait()
    load_amps.wait()

    def spread(zs, xs, high):
        tile = zs * 8 + xs * 2 + high
        for part in range(4):
            for t in range(LANES):
                got = land[zs, xs, high * 2 + part // 2, part % 2, :, t * 128:(t + 1) * 128]
                fa[t, tile, part * 16:(part + 1) * 16] = got
                fa[LANES + t, tile, part * 16:(part + 1) * 16] = jnp.concatenate(
                    [got[:, TILE:], got[:, :TILE]], axis=1
                )

    low = lax.broadcasted_iota(jnp.int32, (TILE, 128), 1) < TILE

    def tile_row(tile, cols):
        got = [fa[col, tile] for col in cols]
        return jnp.concatenate(
            [jnp.where(low, got[0], got[1]), jnp.where(low, got[2], got[3])], axis=1
        )

    def dressed(tile, slot):
        at = tile * SLOTS + slot
        cols = [stab[k, at] for k in range(KEPT)]
        return lax.dot_general(
            tile_row(tile, cols), amps[stab[KEPT, at]], (((1,), (1,)), ((), ())),
            preferred_element_type=jnp.float32,
        )

    def tile_copy(tile, split):
        return pltpu.make_async_remote_copy(
            src_ref=send.at[tile, split], dst_ref=recv_hbm.at[vi, split],
            send_sem=tsend.at[tile * SPLITS + split], recv_sem=trecv.at[vi * SPLITS + split],
            device_id=(zi, tile), device_id_type=MESH,
        )

    def self_copy(split):
        return pltpu.make_async_copy(
            send.at[vi, split], recv_hbm.at[vi, split], tsend.at[vi * SPLITS + split]
        )

    def group(g):
        xs = lax.rem(pos["x"] + 4 - g, 4)

        def mirror(step, carry):
            split = step // 8
            at = lax.rem(step, 8)
            zs, high = lax.rem(pos["x"] + 1 + at // 2, 4), lax.rem(at, 2)
            tile = zs * 8 + xs * 2 + high

            @pl.when(split == 0)
            def _():
                spread(zs, xs, high)

            for s in range(0, PER, 2):
                pair = [dressed(tile, split * PER + s + i).astype(jnp.bfloat16) for i in (0, 1)]
                send[tile, split, s // 2] = jnp.concatenate(pair, axis=1)

            @pl.when(tile != vi)
            def _():
                tile_copy(tile, split).start()

            @pl.when(tile == vi)
            def _():
                self_copy(split).start()

            return carry

        lax.fori_loop(0, 8 * SPLITS, mirror, 0)

    group(0)
    far_third(1)
    far_second(2)
    far_last(1)
    group(1)
    far_third(2)
    far_second(3)
    far_last(2)
    group(2)
    far_third(3)
    far_last(3)
    group(3)

    def own_row(row, carry):
        cols = [sown[k, row] for k in range(KEPT)]
        weights = jnp.concatenate(
            [tile_row(sown[KEPT + k, row], cols) for k in range(KEPT)], axis=0
        )
        own[row] = lax.dot_general(
            amps[row], weights, (((1,), (1,)), ((), ())), preferred_element_type=jnp.float32
        )
        return carry

    lax.fori_loop(0, ROWS, own_row, 0)
    out_copy = pltpu.make_async_copy(own, own_hbm, lsem.at[0])
    out_copy.start()
    for copy in sent:
        copy.wait_send()

    def finish(step, carry):
        peer, split = step // SPLITS, lax.rem(step, SPLITS)

        @pl.when(peer != vi)
        def _():
            tile_copy(peer, split).wait_send()
            pltpu.make_async_remote_copy(
                src_ref=send.at[peer, split], dst_ref=recv_hbm.at[peer, split],
                send_sem=tsend.at[step], recv_sem=trecv.at[step],
                device_id=(zi, peer), device_id_type=MESH,
            ).wait_recv()

        @pl.when(peer == vi)
        def _():
            self_copy(split).wait()

        return carry

    lax.fori_loop(0, NTILES * SPLITS, finish, 0)
    out_copy.wait()


def combine_kernel(back_ref, own_hbm, recv_hbm, out_hbm, own, recv, in_sem, out_sem, recv_sem):
    load_recv = pltpu.make_async_copy(recv_hbm, recv, recv_sem)
    load_recv.start()

    def chunk(number):
        return pl.ds(pl.multiple_of(number * CHUNK, CHUNK), CHUNK)

    def load(number):
        return pltpu.make_async_copy(
            own_hbm.at[chunk(number)], own.at[chunk(number)], in_sem.at[number]
        )

    def store(number):
        return pltpu.make_async_copy(
            own.at[chunk(number)], out_hbm.at[chunk(number)], out_sem.at[number]
        )

    for number in range(ROWS // CHUNK):
        load(number).start()
    load_recv.wait()
    low = lax.broadcasted_iota(jnp.int32, (TILE, 128), 1) < TILE

    def part(number, carry):
        load(number).wait()

        def some_rows(some, carry):
            for r in range(4):
                row = number * CHUNK + some * 4 + r
                for h in range(2):
                    lanes = pl.ds(h * 128, 128)
                    left, right = [recv[back_ref[2 * h + i, row]] for i in range(2)]
                    turns = [back_ref[KEPT + 2 * h + i, row] for i in range(2)]
                    kept = jnp.where(low, left, right)
                    other = jnp.where(low, right, left)
                    other = jnp.concatenate([other[:, TILE:], other[:, :TILE]], axis=1)
                    stay = jnp.where(low, turns[0], turns[1]) == 0
                    own[row, :, lanes] += jnp.where(
                        stay, kept.astype(jnp.float32), other.astype(jnp.float32)
                    )
            return carry

        lax.fori_loop(0, CHUNK // 4, some_rows, 0)
        store(number).start()
        return carry

    lax.fori_loop(0, ROWS // CHUNK, part, 0)
    for number in range(ROWS // CHUNK):
        store(number).wait()


def per_device(amps, fock, cols):
    vmem = pl.BlockSpec(memory_space=pltpu.VMEM)
    smem = pl.BlockSpec(memory_space=pltpu.SMEM)
    anywhere = pl.BlockSpec(memory_space=pl.ANY)
    own, received, back = pl.pallas_call(
        exchange_kernel,
        out_shape=(
            jax.ShapeDtypeStruct((ROWS, TILE, KEPT * TILE), jnp.float32),
            jax.ShapeDtypeStruct((NTILES, SPLITS, PER // 2, TILE, 2 * TILE), jnp.bfloat16),
            jax.ShapeDtypeStruct((2 * KEPT, ROWS), jnp.int32),
        ),
        in_specs=[vmem, vmem, anywhere],
        out_specs=(anywhere, anywhere, vmem),
        scratch_shapes=[
            pltpu.VMEM((4, 4, 4, 2, 16, 2048), jnp.bfloat16),
            pltpu.VMEM((2 * LANES, NTILES, TILE, 128), jnp.bfloat16),
            pltpu.VMEM((ROWS, TILE, KEPT * TILE), jnp.bfloat16),
            pltpu.VMEM((NTILES, SPLITS, PER // 2, TILE, 2 * TILE), jnp.bfloat16),
            pltpu.VMEM((ROWS, TILE, KEPT * TILE), jnp.float32),
            pltpu.VMEM((8, NTILES * SLOTS), jnp.int32),
            pltpu.VMEM((8, ROWS), jnp.int32),
            pltpu.SMEM((8, NTILES * SLOTS), jnp.int32),
            pltpu.SMEM((8, ROWS), jnp.int32),
            pltpu.SemaphoreType.DMA((33,)),
            pltpu.SemaphoreType.DMA((33,)),
            pltpu.SemaphoreType.DMA((20,)),
            pltpu.SemaphoreType.DMA((20,)),
            pltpu.SemaphoreType.DMA((NTILES * SPLITS,)),
            pltpu.SemaphoreType.DMA((NTILES * SPLITS,)),
            pltpu.SemaphoreType.DMA((3,)),
        ],
        compiler_params=pltpu.CompilerParams(
            collective_id=0, has_side_effects=True, vmem_limit_bytes=58 * 2**20
        ),
    )(cols.transpose(0, 2, 1), fock, amps.reshape(ROWS, TILE, KEPT * TILE))
    out = pl.pallas_call(
        combine_kernel,
        out_shape=jax.ShapeDtypeStruct((ROWS, TILE, KEPT * TILE), jnp.float32),
        in_specs=[smem, anywhere, anywhere],
        out_specs=anywhere,
        scratch_shapes=[
            pltpu.VMEM((ROWS, TILE, KEPT * TILE), jnp.float32),
            pltpu.VMEM((NTILES * SLOTS // 2, TILE, 2 * TILE), jnp.bfloat16),
            pltpu.SemaphoreType.DMA((ROWS // CHUNK,)),
            pltpu.SemaphoreType.DMA((ROWS // CHUNK,)),
            pltpu.SemaphoreType.DMA,
        ],
        compiler_params=pltpu.CompilerParams(vmem_limit_bytes=58 * 2**20),
    )(back, own, received.reshape(NTILES * SLOTS // 2, TILE, 2 * TILE))
    return out[None]


def solution(mesh):
    in_specs = (P("virt", "pairs", None, None), P(("pairs", "virt"), None), P(None, "pairs", None))
    out_specs = P("virt", "pairs", None, None)
    return jax.shard_map(
        per_device, mesh=mesh, in_specs=in_specs, out_specs=out_specs, check_vma=False
    )
```

```python
import functools

import jax
import jax.numpy as jnp
from jax import lax
from jax.experimental import pallas as pl
from jax.experimental.pallas import tpu as pltpu
from jax.sharding import PartitionSpec as P

MESH = pl.DeviceIdType.MESH
TILE = 64
KEPT = 4
ROWS = 128
NTILES = 32
NSIDE = 4
SPLITS = 4
SLOTS = 32
PER = SLOTS // SPLITS
LANES = 16
CHUNK = 16
HALF = 1024


def place(pos):
    return (pos["z"], pos["x"] * 8 + pos["y"] * 2 + pos["c"])


def moved(pos, axis, by):
    new = dict(pos)
    new[axis] = lax.rem(pos[axis] + by + 4, 4)
    return new


def write_tables(me, cols_ref, vtab, vown, back_ref):
    f32, bf16, i32 = jnp.float32, jnp.bfloat16, jnp.int32
    mine = cols_ref[me]
    kept = lax.broadcasted_iota(i32, (KEPT, ROWS), 0)
    lane = lax.broadcasted_iota(i32, (KEPT, ROWS), 1)
    mine = jnp.minimum(jnp.maximum(mine, 0), NTILES - 1)
    spot = ((mine + kept) & 1) * LANES + (mine >> 1)
    vown[...] = jnp.concatenate([spot, mine], axis=0)
    first = lax.broadcasted_iota(i32, (ROWS, ROWS), 0)
    second = lax.broadcasted_iota(i32, (ROWS, ROWS), 1)
    upper = (first <= second).astype(f32).astype(bf16)
    flip = (first + second == ROWS - 1).astype(f32).astype(bf16)
    about = jnp.concatenate([spot, lane], axis=0).astype(f32).astype(bf16)
    about = jnp.dot(about, flip, preferred_element_type=f32).astype(bf16)
    named = jnp.sum((cols_ref[...] == me).astype(f32), axis=1)
    upto = jnp.dot(named.astype(bf16), upper, preferred_element_type=f32)
    rank = jnp.where(named > 0, upto, 0.0)
    slots = lax.broadcasted_iota(i32, (SLOTS, ROWS), 0).astype(f32) + 1.0
    entry = lax.broadcasted_iota(i32, (8, 8 * SLOTS), 0)
    largest = jnp.where(entry < KEPT, 2 * LANES - 1, ROWS - 1)
    for peer in range(0, NTILES, 8):
        hot = [
            (jnp.broadcast_to(rank[p:p + 1], (SLOTS, ROWS)) == slots).astype(f32).astype(bf16)
            for p in range(peer, peer + 8)
        ]
        got = lax.dot_general(
            about, jnp.concatenate(hot, axis=0), (((1,), (1,)), ((), ())),
            preferred_element_type=f32,
        )
        got = jnp.minimum(jnp.maximum(got.astype(i32), 0), largest)
        vtab[:, peer * SLOTS:(peer + 8) * SLOTS] = got
    number = lax.broadcasted_iota(i32, (NTILES, ROWS), 0)
    at = [jnp.broadcast_to(mine[k:k + 1], (NTILES, ROWS)) == number for k in range(KEPT)]
    count = sum(hit.astype(f32) for hit in at)
    before = jnp.dot(count.astype(bf16), upper, preferred_element_type=f32) - count
    slot = [jnp.sum(jnp.where(hit, before, 0.0), axis=0, keepdims=True) for hit in at]
    slot = jnp.minimum(jnp.maximum(jnp.concatenate(slot, axis=0).astype(i32), 0), SLOTS - 1)
    back_ref[...] = jnp.concatenate(
        [mine * (SLOTS // 2) + (slot >> 1), ((slot + kept) & 1) * TILE], axis=0
    )


def exchange_kernel(
    cols_ref, fock_ref, amps_hbm, own, recv, back_ref,
    land, fa, amps, send, vtab, vown, stab, sown,
    gsend, grecv, csend, crecv, tsend, trecv, lsem,
):
    zi = lax.axis_index("pairs")
    vi = lax.axis_index("virt")
    pos = {"x": vi // 8, "y": lax.rem(vi // 2, 4), "z": zi, "c": lax.rem(vi, 2)}
    twin = {**pos, "c": 1 - pos["c"]}

    load_amps = pltpu.make_async_copy(amps_hbm, amps, lsem.at[0])
    load_amps.start()

    barrier = pltpu.get_barrier_semaphore()

    def greet(off, carry):
        pl.semaphore_signal(
            barrier, inc=1, device_id=(zi, lax.rem(vi + off, NTILES)), device_id_type=MESH
        )
        return carry

    lax.fori_loop(1, NTILES, greet, 0)
    for by in (1, 2, 3):
        pl.semaphore_signal(
            barrier, inc=1, device_id=place(moved(pos, "z", by)), device_id_type=MESH
        )
    land[pos["z"], pos["x"], pos["y"], pos["c"]] = fock_ref[...]
    pl.semaphore_wait(barrier, NTILES - 1 + 3)

    sent = []

    def rows_at(where, full, half):
        at = [slice(None) if axis in full else where[axis] for axis in "zxy"]
        cols = slice(None) if half is None else pl.ds(half * HALF, HALF)
        return land.at[at[0], at[1], at[2], where["c"], :, cols]

    def copy_to(target, number, src, dst, out=gsend, into=grecv):
        return pltpu.make_async_remote_copy(
            src_ref=src, dst_ref=dst, send_sem=out.at[number], recv_sem=into.at[number],
            device_id=place(target), device_id_type=MESH,
        )

    def push(axis, by, number, where, full="", half=None, own_rows=False):
        dst = rows_at(where, full, half)
        src = dst
        if own_rows:
            src = fock_ref if half is None else fock_ref.at[:, pl.ds(half * HALF, HALF)]
        copy = copy_to(moved(pos, axis, by), number, src, dst)
        copy.start()
        sent.append(copy)

    def arrived(number, where, full="", half=None):
        ref = rows_at(where, full, half)
        copy_to(twin, number, ref, ref).wait_recv()

    def across(number, where, full="", half=None):
        ref = rows_at(where, full, half)
        copy = copy_to(twin, number, ref, ref, csend, crecv)
        copy.start()
        sent.append(copy)

    def came_across(number, where, full="", half=None):
        ref = rows_at({**where, "c": twin["c"]}, full, half)
        copy_to(twin, number, ref, ref, csend, crecv).wait_recv()

    def far(g):
        return moved(pos, "x", -g)

    def far_first(g):
        arrived(g - 1, far(g))
        for by in (1, 2, 3):
            push("y", by, 15 + 6 * (g - 1) + by - 1, far(g))

    def far_second(g):
        for by in (1, 2, 3):
            arrived(15 + 6 * (g - 1) + by - 1, moved(far(g), "y", -by))
        for by in (1, 2, 3):
            push("z", by, 18 + 6 * (g - 1) + by - 1, far(g), "y")
        across(8 + 4 * (g - 1), far(g), "y")

    def far_third(g):
        for by in (1, 2, 3):
            there = moved(far(g), "z", -by)
            arrived(18 + 6 * (g - 1) + by - 1, there, "y")
            across(8 + 4 * (g - 1) + by, there, "y")

    def far_last(g):
        for by in range(4):
            came_across(8 + 4 * (g - 1) + by, moved(far(g), "z", -by), "y")

    for by in (1, 2, 3):
        push("z", by, 3 + by - 1, pos, half=0, own_rows=True)
        push("y", by, 6 + by - 1, pos, half=1, own_rows=True)
    for by in (1, 2, 3):
        push("x", by, by - 1, pos, own_rows=True)
    write_tables(vi, cols_ref, vtab, vown, back_ref)
    job_table = pltpu.make_async_copy(vtab, stab, lsem.at[1])
    own_table = pltpu.make_async_copy(vown, sown, lsem.at[2])
    job_table.start()
    own_table.start()
    for half, axis, other in ((0, "z", "y"), (1, "y", "z")):
        for by in (1, 2, 3):
            arrived(3 + 3 * half + by - 1, moved(pos, axis, -by), half=half)
        for by in (1, 2, 3):
            push(other, by, 9 + 3 * half + by - 1, pos, axis, half)
        across(4 * half, pos, axis, half)
    for g in (1, 2, 3):
        far_first(g)
    for by in (1, 2, 3):
        for half, axis, other in ((0, "z", "y"), (1, "y", "z")):
            there = moved(pos, other, -by)
            arrived(9 + 3 * half + by - 1, there, axis, half)
            across(4 * half + by, there, axis, half)
    far_second(1)
    for by in range(4):
        for half, axis, other in ((0, "z", "y"), (1, "y", "z")):
            came_across(4 * half + by, moved(pos, other, -by), axis, half)
    job_table.wait()
    own_table.wait()
    load_amps.wait()

    def spread(zs, xs, high):
        tile = zs * 8 + xs * 2 + high
        for part in range(4):
            for t in range(LANES):
                got = land[zs, xs, high * 2 + part // 2, part % 2, :, t * 128:(t + 1) * 128]
                fa[t, tile, part * 16:(part + 1) * 16] = got
                fa[LANES + t, tile, part * 16:(part + 1) * 16] = jnp.concatenate(
                    [got[:, TILE:], got[:, :TILE]], axis=1
                )

    low = lax.broadcasted_iota(jnp.int32, (TILE, 128), 1) < TILE

    def tile_row(tile, cols):
        got = [fa[col, tile] for col in cols]
        return jnp.concatenate(
            [jnp.where(low, got[0], got[1]), jnp.where(low, got[2], got[3])], axis=1
        )

    def dressed(tile, slot):
        at = tile * SLOTS + slot
        cols = [stab[k, at] for k in range(KEPT)]
        return lax.dot_general(
            tile_row(tile, cols), amps[stab[KEPT, at]], (((1,), (1,)), ((), ())),
            preferred_element_type=jnp.float32,
        )

    def tile_copy(tile, split):
        return pltpu.make_async_remote_copy(
            src_ref=send.at[tile, split], dst_ref=recv.at[vi, split],
            send_sem=tsend.at[tile * SPLITS + split], recv_sem=trecv.at[vi * SPLITS + split],
            device_id=(zi, tile), device_id_type=MESH,
        )

    def self_copy(split):
        return pltpu.make_async_copy(
            send.at[vi, split], recv.at[vi, split], tsend.at[vi * SPLITS + split]
        )

    def group(g):
        xs = lax.rem(pos["x"] + 4 - g, 4)

        def mirror(step, carry):
            split = step // 8
            at = lax.rem(step, 8)
            turn = 3 * lax.rem(at, 4) + 2 * (at // 4) + pos["y"] + 2 * pos["c"]
            zs, high = lax.rem(pos["x"] + turn, 4), lax.rem(at // 4 + pos["c"], 2)
            tile = zs * 8 + xs * 2 + high

            @pl.when(split == 0)
            def _():
                spread(zs, xs, high)

            for s in range(0, PER, 2):
                pair = [dressed(tile, split * PER + s + i).astype(jnp.bfloat16) for i in (0, 1)]
                send[tile, split, s // 2] = jnp.concatenate(pair, axis=1)

            @pl.when(tile != vi)
            def _():
                tile_copy(tile, split).start()

            @pl.when(tile == vi)
            def _():
                self_copy(split).start()

            return carry

        lax.fori_loop(0, 8 * SPLITS, mirror, 0)

    group(0)
    far_third(1)
    far_second(2)
    far_last(1)
    group(1)
    far_third(2)
    far_second(3)
    far_last(2)
    group(2)
    far_third(3)
    far_last(3)
    group(3)

    def own_row(row, carry):
        cols = [sown[k, row] for k in range(KEPT)]
        weights = jnp.concatenate(
            [tile_row(sown[KEPT + k, row], cols) for k in range(KEPT)], axis=0
        )
        own[row] = lax.dot_general(
            amps[row], weights, (((1,), (1,)), ((), ())), preferred_element_type=jnp.float32
        )
        return carry

    lax.fori_loop(0, ROWS, own_row, 0)
    for copy in sent:
        copy.wait_send()

    def finish(step, carry):
        peer, split = step // SPLITS, lax.rem(step, SPLITS)

        @pl.when(peer != vi)
        def _():
            tile_copy(peer, split).wait_send()
            pltpu.make_async_remote_copy(
                src_ref=send.at[peer, split], dst_ref=recv.at[peer, split],
                send_sem=tsend.at[step], recv_sem=trecv.at[step],
                device_id=(zi, peer), device_id_type=MESH,
            ).wait_recv()

        @pl.when(peer == vi)
        def _():
            self_copy(split).wait()

        return carry

    lax.fori_loop(0, NTILES * SPLITS, finish, 0)


def combine_kernel(back_ref, own, recv, out_hbm, out, out_sem):
    def store(number):
        part = pl.ds(pl.multiple_of(number * CHUNK, CHUNK), CHUNK)
        return pltpu.make_async_copy(out.at[part], out_hbm.at[part], out_sem.at[number])

    low = lax.broadcasted_iota(jnp.int32, (TILE, 128), 1) < TILE

    def part(number, carry):
        def some_rows(some, carry):
            for r in range(4):
                row = number * CHUNK + some * 4 + r
                for h in range(2):
                    lanes = pl.ds(h * 128, 128)
                    left, right = [recv[back_ref[2 * h + i, row]] for i in range(2)]
                    turns = [back_ref[KEPT + 2 * h + i, row] for i in range(2)]
                    kept = jnp.where(low, left, right)
                    other = jnp.where(low, right, left)
                    other = jnp.concatenate([other[:, TILE:], other[:, :TILE]], axis=1)
                    stay = jnp.where(low, turns[0], turns[1]) == 0
                    out[row, :, lanes] = own[row, :, lanes] + jnp.where(
                        stay, kept.astype(jnp.float32), other.astype(jnp.float32)
                    )
            return carry

        lax.fori_loop(0, CHUNK // 4, some_rows, 0)
        store(number).start()
        return carry

    lax.fori_loop(0, ROWS // CHUNK, part, 0)
    for number in range(ROWS // CHUNK):
        store(number).wait()


def per_device(amps, fock, cols):
    vmem = pl.BlockSpec(memory_space=pltpu.VMEM)
    smem = pl.BlockSpec(memory_space=pltpu.SMEM)
    anywhere = pl.BlockSpec(memory_space=pl.ANY)
    own, received, back = pl.pallas_call(
        exchange_kernel,
        out_shape=(
            pltpu.VMEM((ROWS, TILE, KEPT * TILE), jnp.float32),
            pltpu.VMEM((NTILES, SPLITS, PER // 2, TILE, 2 * TILE), jnp.bfloat16),
            jax.ShapeDtypeStruct((2 * KEPT, ROWS), jnp.int32),
        ),
        in_specs=[vmem, vmem, anywhere],
        out_specs=(vmem, vmem, vmem),
        scratch_shapes=[
            pltpu.VMEM((4, 4, 4, 2, 16, 2048), jnp.bfloat16),
            pltpu.VMEM((2 * LANES, NTILES, TILE, 128), jnp.bfloat16),
            pltpu.VMEM((ROWS, TILE, KEPT * TILE), jnp.bfloat16),
            pltpu.VMEM((NTILES, SPLITS, PER // 2, TILE, 2 * TILE), jnp.bfloat16),
            pltpu.VMEM((8, NTILES * SLOTS), jnp.int32),
            pltpu.VMEM((8, ROWS), jnp.int32),
            pltpu.SMEM((8, NTILES * SLOTS), jnp.int32),
            pltpu.SMEM((8, ROWS), jnp.int32),
            pltpu.SemaphoreType.DMA((33,)),
            pltpu.SemaphoreType.DMA((33,)),
            pltpu.SemaphoreType.DMA((20,)),
            pltpu.SemaphoreType.DMA((20,)),
            pltpu.SemaphoreType.DMA((NTILES * SPLITS,)),
            pltpu.SemaphoreType.DMA((NTILES * SPLITS,)),
            pltpu.SemaphoreType.DMA((3,)),
        ],
        compiler_params=pltpu.CompilerParams(
            collective_id=0, has_side_effects=True, vmem_limit_bytes=42 * 2**20
        ),
    )(cols.transpose(0, 2, 1), fock, amps.reshape(ROWS, TILE, KEPT * TILE))
    out = pl.pallas_call(
        combine_kernel,
        out_shape=jax.ShapeDtypeStruct((ROWS, TILE, KEPT * TILE), jnp.float32),
        in_specs=[smem, vmem, vmem],
        out_specs=anywhere,
        scratch_shapes=[
            pltpu.VMEM((ROWS, TILE, KEPT * TILE), jnp.float32),
            pltpu.SemaphoreType.DMA((ROWS // CHUNK,)),
        ],
        compiler_params=pltpu.CompilerParams(vmem_limit_bytes=12 * 2**20),
    )(back, own, received.reshape(NTILES * SLOTS // 2, TILE, 2 * TILE))
    return out[None]


def solution(mesh):
    in_specs = (P("virt", "pairs", None, None), P(("pairs", "virt"), None), P(None, "pairs", None))
    out_specs = P("virt", "pairs", None, None)
    return jax.shard_map(
        per_device, mesh=mesh, in_specs=in_specs, out_specs=out_specs, check_vma=False
    )
```

```python
import functools

import jax
import jax.numpy as jnp
from jax import lax
from jax.experimental import pallas as pl
from jax.experimental.pallas import tpu as pltpu
from jax.sharding import PartitionSpec as P

MESH = pl.DeviceIdType.MESH
TILE = 64
KEPT = 4
ROWS = 128
NTILES = 32
NSIDE = 4
SPLITS = 4
SLOTS = 32
PER = SLOTS // SPLITS
LANES = 16
CHUNK = 16
HALF = 1024


def place(pos):
    return (pos["z"], pos["x"] * 8 + pos["y"] * 2 + pos["c"])


def moved(pos, axis, by):
    new = dict(pos)
    new[axis] = lax.rem(pos[axis] + by + 4, 4)
    return new


def write_tables(me, cols_ref, vtab, vown, back_ref):
    f32, bf16, i32 = jnp.float32, jnp.bfloat16, jnp.int32
    mine = cols_ref[me]
    kept = lax.broadcasted_iota(i32, (KEPT, ROWS), 0)
    lane = lax.broadcasted_iota(i32, (KEPT, ROWS), 1)
    mine = jnp.minimum(jnp.maximum(mine, 0), NTILES - 1)
    spot = ((mine + kept) & 1) * LANES + (mine >> 1)
    vown[...] = jnp.concatenate([spot, mine], axis=0)
    first = lax.broadcasted_iota(i32, (ROWS, ROWS), 0)
    second = lax.broadcasted_iota(i32, (ROWS, ROWS), 1)
    upper = (first <= second).astype(f32).astype(bf16)
    flip = (first + second == ROWS - 1).astype(f32).astype(bf16)
    about = jnp.concatenate([spot, lane], axis=0).astype(f32).astype(bf16)
    about = jnp.dot(about, flip, preferred_element_type=f32).astype(bf16)
    named = jnp.sum((cols_ref[...] == me).astype(f32), axis=1)
    upto = jnp.dot(named.astype(bf16), upper, preferred_element_type=f32)
    rank = jnp.where(named > 0, upto, 0.0)
    slots = lax.broadcasted_iota(i32, (SLOTS, ROWS), 0).astype(f32) + 1.0
    entry = lax.broadcasted_iota(i32, (8, 8 * SLOTS), 0)
    largest = jnp.where(entry < KEPT, 2 * LANES - 1, ROWS - 1)
    for peer in range(0, NTILES, 8):
        hot = [
            (jnp.broadcast_to(rank[p:p + 1], (SLOTS, ROWS)) == slots).astype(f32).astype(bf16)
            for p in range(peer, peer + 8)
        ]
        got = lax.dot_general(
            about, jnp.concatenate(hot, axis=0), (((1,), (1,)), ((), ())),
            preferred_element_type=f32,
        )
        got = jnp.minimum(jnp.maximum(got.astype(i32), 0), largest)
        vtab[:, peer * SLOTS:(peer + 8) * SLOTS] = got
    number = lax.broadcasted_iota(i32, (NTILES, ROWS), 0)
    at = [jnp.broadcast_to(mine[k:k + 1], (NTILES, ROWS)) == number for k in range(KEPT)]
    count = sum(hit.astype(f32) for hit in at)
    before = jnp.dot(count.astype(bf16), upper, preferred_element_type=f32) - count
    slot = [jnp.sum(jnp.where(hit, before, 0.0), axis=0, keepdims=True) for hit in at]
    slot = jnp.minimum(jnp.maximum(jnp.concatenate(slot, axis=0).astype(i32), 0), SLOTS - 1)
    back_ref[...] = jnp.concatenate(
        [mine * (SLOTS // 2) + (slot >> 1), ((slot + kept) & 1) * TILE], axis=0
    )


def exchange_kernel(
    cols_hbm, fock_ref, amps_hbm, own, recv, back_ref,
    land, fa, amps, send, cols_ref, vtab, vown, stab, sown,
    gsend, grecv, csend, crecv, tsend, trecv, lsem,
):
    zi = lax.axis_index("pairs")
    vi = lax.axis_index("virt")
    pos = {"x": vi // 8, "y": lax.rem(vi // 2, 4), "z": zi, "c": lax.rem(vi, 2)}
    twin = {**pos, "c": 1 - pos["c"]}

    load_amps = pltpu.make_async_copy(amps_hbm, amps, lsem.at[0])

    barrier = pltpu.get_barrier_semaphore()

    def greet(off, carry):
        pl.semaphore_signal(
            barrier, inc=1, device_id=(zi, lax.rem(vi + off, NTILES)), device_id_type=MESH
        )
        return carry

    for off in range(1, NTILES):
        greet(off, 0)
    for by in (1, 2, 3):
        pl.semaphore_signal(
            barrier, inc=1, device_id=place(moved(pos, "z", by)), device_id_type=MESH
        )
    load_cols = pltpu.make_async_copy(cols_hbm, cols_ref, lsem.at[1])
    load_cols.start()
    load_amps.start()
    load_rows = pltpu.make_async_copy(
        fock_ref, land.at[pos["z"], pos["x"], pos["y"], pos["c"]], lsem.at[2]
    )
    load_rows.start()
    load_rows.wait()
    pl.semaphore_wait(barrier, NTILES - 1 + 3)

    sent = []

    def rows_at(where, full, half):
        at = [slice(None) if axis in full else where[axis] for axis in "zxy"]
        cols = slice(None) if half is None else pl.ds(half * HALF, HALF)
        return land.at[at[0], at[1], at[2], where["c"], :, cols]

    def copy_to(target, number, src, dst, out=gsend, into=grecv):
        return pltpu.make_async_remote_copy(
            src_ref=src, dst_ref=dst, send_sem=out.at[number], recv_sem=into.at[number],
            device_id=place(target), device_id_type=MESH,
        )

    def push(axis, by, number, where, full="", half=None):
        ref = rows_at(where, full, half)
        copy = copy_to(moved(pos, axis, by), number, ref, ref)
        copy.start()
        sent.append(copy)

    def arrived(number, where, full="", half=None):
        ref = rows_at(where, full, half)
        copy_to(twin, number, ref, ref).wait_recv()

    def across(number, where, full="", half=None):
        ref = rows_at(where, full, half)
        copy = copy_to(twin, number, ref, ref, csend, crecv)
        copy.start()
        sent.append(copy)

    def came_across(number, where, full="", half=None):
        ref = rows_at({**where, "c": twin["c"]}, full, half)
        copy_to(twin, number, ref, ref, csend, crecv).wait_recv()

    def far(g):
        return moved(pos, "x", -g)

    def far_first(g):
        arrived(g - 1, far(g), half=0)
        for by in (1, 2, 3):
            push("y", by, 15 + 6 * (g - 1) + by - 1, far(g), half=0)

    def far_second(g):
        for by in (1, 2, 3):
            arrived(15 + 6 * (g - 1) + by - 1, moved(far(g), "y", -by), half=0)
        arrived(32 + g, far(g), "y", half=1)
        for by in (1, 2, 3):
            push("z", by, 18 + 6 * (g - 1) + by - 1, far(g), "y")
        across(8 + 4 * (g - 1), far(g), "y")

    def far_third(g):
        for by in (1, 2, 3):
            there = moved(far(g), "z", -by)
            arrived(18 + 6 * (g - 1) + by - 1, there, "y")
            across(8 + 4 * (g - 1) + by, there, "y")

    def far_last(g):
        for by in range(4):
            came_across(8 + 4 * (g - 1) + by, moved(far(g), "z", -by), "y")

    for by in (1, 2, 3):
        push("z", by, 3 + by - 1, pos, half=0)
        push("y", by, 6 + by - 1, pos, half=1)
    for by in (1, 2, 3):
        push("x", by, by - 1, pos, half=0)
    load_cols.wait()
    write_tables(vi, cols_ref, vtab, vown, back_ref)
    job_table = pltpu.make_async_copy(vtab, stab, lsem.at[1])
    own_table = pltpu.make_async_copy(vown, sown, lsem.at[2])
    job_table.start()
    own_table.start()
    for half, axis, other in ((0, "z", "y"), (1, "y", "z")):
        for by in (1, 2, 3):
            arrived(3 + 3 * half + by - 1, moved(pos, axis, -by), half=half)
        for by in (1, 2, 3):
            push(other, by, 9 + 3 * half + by - 1, pos, axis, half)
        across(4 * half, pos, axis, half)
    for by in (1, 2, 3):
        push("x", by, 32 + by, pos, "y", half=1)
    for g in (1, 2, 3):
        far_first(g)
    for by in (1, 2, 3):
        for half, axis, other in ((0, "z", "y"), (1, "y", "z")):
            there = moved(pos, other, -by)
            arrived(9 + 3 * half + by - 1, there, axis, half)
            across(4 * half + by, there, axis, half)
    far_second(1)
    for by in range(4):
        for half, axis, other in ((0, "z", "y"), (1, "y", "z")):
            came_across(4 * half + by, moved(pos, other, -by), axis, half)
    job_table.wait()
    own_table.wait()
    load_amps.wait()

    def spread(zs, xs, high):
        tile = zs * 8 + xs * 2 + high
        for part in range(4):
            for t in range(LANES):
                got = land[zs, xs, high * 2 + part // 2, part % 2, :, t * 128:(t + 1) * 128]
                fa[t, tile, part * 16:(part + 1) * 16] = got
                fa[LANES + t, tile, part * 16:(part + 1) * 16] = jnp.concatenate(
                    [got[:, TILE:], got[:, :TILE]], axis=1
                )

    low = lax.broadcasted_iota(jnp.int32, (TILE, 128), 1) < TILE

    def tile_row(tile, cols):
        got = [fa[col, tile] for col in cols]
        return jnp.concatenate(
            [jnp.where(low, got[0], got[1]), jnp.where(low, got[2], got[3])], axis=1
        )

    def dressed(tile, slot):
        at = tile * SLOTS + slot
        cols = [stab[k, at] for k in range(KEPT)]
        return lax.dot_general(
            tile_row(tile, cols), amps[stab[KEPT, at]], (((1,), (1,)), ((), ())),
            preferred_element_type=jnp.float32,
        )

    def tile_copy(tile, split):
        return pltpu.make_async_remote_copy(
            src_ref=send.at[tile, split], dst_ref=recv.at[vi, split],
            send_sem=tsend.at[tile * SPLITS + split], recv_sem=trecv.at[vi * SPLITS + split],
            device_id=(zi, tile), device_id_type=MESH,
        )

    def self_copy(split):
        return pltpu.make_async_copy(
            send.at[vi, split], recv.at[vi, split], tsend.at[vi * SPLITS + split]
        )

    def group(g):
        xs = lax.rem(pos["x"] + 4 - g, 4)

        def mirror(step, carry):
            split = step // 8
            at = lax.rem(step, 8)
            turn = 3 * lax.rem(at, 4) + 2 * (at // 4) + pos["y"] + 2 * pos["c"]
            zs, high = lax.rem(pos["x"] + turn, 4), lax.rem(at // 4 + pos["c"], 2)
            tile = zs * 8 + xs * 2 + high

            @pl.when(split == 0)
            def _():
                spread(zs, xs, high)

            for s in range(0, PER, 2):
                pair = [dressed(tile, split * PER + s + i).astype(jnp.bfloat16) for i in (0, 1)]
                send[tile, split, s // 2] = jnp.concatenate(pair, axis=1)

            @pl.when(tile != vi)
            def _():
                tile_copy(tile, split).start()

            @pl.when(tile == vi)
            def _():
                self_copy(split).start()

            return carry

        lax.fori_loop(0, 8 * SPLITS, mirror, 0)

    group(0)
    far_third(1)
    far_second(2)
    far_last(1)
    group(1)
    far_third(2)
    far_second(3)
    far_last(2)
    group(2)
    far_third(3)
    far_last(3)
    group(3)

    def own_row(row, carry):
        cols = [sown[k, row] for k in range(KEPT)]
        weights = jnp.concatenate(
            [tile_row(sown[KEPT + k, row], cols) for k in range(KEPT)], axis=0
        )
        own[row] = lax.dot_general(
            amps[row], weights, (((1,), (1,)), ((), ())), preferred_element_type=jnp.float32
        )
        return carry

    lax.fori_loop(0, ROWS, own_row, 0)
    for copy in sent:
        copy.wait_send()

    def finish(step, carry):
        peer, split = step // SPLITS, lax.rem(step, SPLITS)

        @pl.when(peer != vi)
        def _():
            tile_copy(peer, split).wait_send()
            pltpu.make_async_remote_copy(
                src_ref=send.at[peer, split], dst_ref=recv.at[peer, split],
                send_sem=tsend.at[step], recv_sem=trecv.at[step],
                device_id=(zi, peer), device_id_type=MESH,
            ).wait_recv()

        @pl.when(peer == vi)
        def _():
            self_copy(split).wait()

        return carry

    lax.fori_loop(0, NTILES * SPLITS, finish, 0)


def combine_kernel(back_ref, own, recv, out_hbm, out, out_sem):
    def store(number):
        part = pl.ds(pl.multiple_of(number * CHUNK, CHUNK), CHUNK)
        return pltpu.make_async_copy(out.at[part], out_hbm.at[part], out_sem.at[number])

    low = lax.broadcasted_iota(jnp.int32, (TILE, 128), 1) < TILE

    def part(number, carry):
        def some_rows(some, carry):
            for r in range(4):
                row = number * CHUNK + some * 4 + r
                for h in range(2):
                    lanes = pl.ds(h * 128, 128)
                    left, right = [recv[back_ref[2 * h + i, row]] for i in range(2)]
                    turns = [back_ref[KEPT + 2 * h + i, row] for i in range(2)]
                    kept = jnp.where(low, left, right)
                    other = jnp.where(low, right, left)
                    other = jnp.concatenate([other[:, TILE:], other[:, :TILE]], axis=1)
                    stay = jnp.where(low, turns[0], turns[1]) == 0
                    out[row, :, lanes] = own[row, :, lanes] + jnp.where(
                        stay, kept.astype(jnp.float32), other.astype(jnp.float32)
                    )
            return carry

        lax.fori_loop(0, CHUNK // 4, some_rows, 0)
        store(number).start()
        return carry

    lax.fori_loop(0, ROWS // CHUNK, part, 0)
    for number in range(ROWS // CHUNK):
        store(number).wait()


def per_device(amps, fock, cols):
    vmem = pl.BlockSpec(memory_space=pltpu.VMEM)
    smem = pl.BlockSpec(memory_space=pltpu.SMEM)
    anywhere = pl.BlockSpec(memory_space=pl.ANY)
    own, received, back = pl.pallas_call(
        exchange_kernel,
        out_shape=(
            pltpu.VMEM((ROWS, TILE, KEPT * TILE), jnp.float32),
            pltpu.VMEM((NTILES, SPLITS, PER // 2, TILE, 2 * TILE), jnp.bfloat16),
            jax.ShapeDtypeStruct((2 * KEPT, ROWS), jnp.int32),
        ),
        in_specs=[anywhere, anywhere, anywhere],
        out_specs=(vmem, vmem, vmem),
        scratch_shapes=[
            pltpu.VMEM((4, 4, 4, 2, 16, 2048), jnp.bfloat16),
            pltpu.VMEM((2 * LANES, NTILES, TILE, 128), jnp.bfloat16),
            pltpu.VMEM((ROWS, TILE, KEPT * TILE), jnp.bfloat16),
            pltpu.VMEM((NTILES, SPLITS, PER // 2, TILE, 2 * TILE), jnp.bfloat16),
            pltpu.VMEM((NTILES, KEPT, ROWS), jnp.int32),
            pltpu.VMEM((8, NTILES * SLOTS), jnp.int32),
            pltpu.VMEM((8, ROWS), jnp.int32),
            pltpu.SMEM((8, NTILES * SLOTS), jnp.int32),
            pltpu.SMEM((8, ROWS), jnp.int32),
            pltpu.SemaphoreType.DMA((36,)),
            pltpu.SemaphoreType.DMA((36,)),
            pltpu.SemaphoreType.DMA((20,)),
            pltpu.SemaphoreType.DMA((20,)),
            pltpu.SemaphoreType.DMA((NTILES * SPLITS,)),
            pltpu.SemaphoreType.DMA((NTILES * SPLITS,)),
            pltpu.SemaphoreType.DMA((3,)),
        ],
        compiler_params=pltpu.CompilerParams(
            collective_id=0, has_side_effects=True, vmem_limit_bytes=42 * 2**20
        ),
    )(cols.transpose(0, 2, 1), fock, amps.reshape(ROWS, TILE, KEPT * TILE))
    out = pl.pallas_call(
        combine_kernel,
        out_shape=jax.ShapeDtypeStruct((ROWS, TILE, KEPT * TILE), jnp.float32),
        in_specs=[smem, vmem, vmem],
        out_specs=anywhere,
        scratch_shapes=[
            pltpu.VMEM((ROWS, TILE, KEPT * TILE), jnp.float32),
            pltpu.SemaphoreType.DMA((ROWS // CHUNK,)),
        ],
        compiler_params=pltpu.CompilerParams(vmem_limit_bytes=12 * 2**20),
    )(back, own, received.reshape(NTILES * SLOTS // 2, TILE, 2 * TILE))
    return out[None]


def solution(mesh):
    in_specs = (P("virt", "pairs", None, None), P(("pairs", "virt"), None), P(None, "pairs", None))
    out_specs = P("virt", "pairs", None, None)
    return jax.shard_map(
        per_device, mesh=mesh, in_specs=in_specs, out_specs=out_specs, check_vma=False
    )
```

```python
import functools

import jax
import jax.numpy as jnp
from jax import lax
from jax.experimental import pallas as pl
from jax.experimental.pallas import tpu as pltpu
from jax.sharding import PartitionSpec as P

MESH = pl.DeviceIdType.MESH
TILE = 64
KEPT = 4
ROWS = 128
NTILES = 32
NSIDE = 4
SPLITS = 4
SLOTS = 32
PER = SLOTS // SPLITS
LANES = 16
CHUNK = 8
HALF = 1024


def place(pos):
    return (pos["z"], pos["x"] * 8 + pos["y"] * 2 + pos["c"])


def moved(pos, axis, by):
    new = dict(pos)
    new[axis] = lax.rem(pos[axis] + by + 4, 4)
    return new


def write_tables(me, cols_ref, vtab, vown, back_ref):
    f32, bf16, i32 = jnp.float32, jnp.bfloat16, jnp.int32
    mine = cols_ref[me]
    kept = lax.broadcasted_iota(i32, (KEPT, ROWS), 0)
    lane = lax.broadcasted_iota(i32, (KEPT, ROWS), 1)
    mine = jnp.minimum(jnp.maximum(mine, 0), NTILES - 1)
    spot = ((mine + kept) & 1) * LANES + (mine >> 1)
    vown[...] = jnp.concatenate([spot, mine], axis=0)
    first = lax.broadcasted_iota(i32, (ROWS, ROWS), 0)
    second = lax.broadcasted_iota(i32, (ROWS, ROWS), 1)
    upper = (first <= second).astype(f32).astype(bf16)
    flip = (first + second == ROWS - 1).astype(f32).astype(bf16)
    about = jnp.concatenate([spot, lane], axis=0).astype(f32).astype(bf16)
    about = jnp.dot(about, flip, preferred_element_type=f32).astype(bf16)
    named = jnp.sum((cols_ref[...] == me).astype(f32), axis=1)
    upto = jnp.dot(named.astype(bf16), upper, preferred_element_type=f32)
    rank = jnp.where(named > 0, upto, 0.0)
    slots = lax.broadcasted_iota(i32, (SLOTS, ROWS), 0).astype(f32) + 1.0
    entry = lax.broadcasted_iota(i32, (8, 8 * SLOTS), 0)
    largest = jnp.where(entry < KEPT, 2 * LANES - 1, ROWS - 1)
    for peer in range(0, NTILES, 8):
        hot = [
            (jnp.broadcast_to(rank[p:p + 1], (SLOTS, ROWS)) == slots).astype(f32).astype(bf16)
            for p in range(peer, peer + 8)
        ]
        got = lax.dot_general(
            about, jnp.concatenate(hot, axis=0), (((1,), (1,)), ((), ())),
            preferred_element_type=f32,
        )
        got = jnp.minimum(jnp.maximum(got.astype(i32), 0), largest)
        vtab[:, peer * SLOTS:(peer + 8) * SLOTS] = got
    number = lax.broadcasted_iota(i32, (NTILES, ROWS), 0)
    at = [jnp.broadcast_to(mine[k:k + 1], (NTILES, ROWS)) == number for k in range(KEPT)]
    count = sum(hit.astype(f32) for hit in at)
    before = jnp.dot(count.astype(bf16), upper, preferred_element_type=f32) - count
    slot = [jnp.sum(jnp.where(hit, before, 0.0), axis=0, keepdims=True) for hit in at]
    slot = jnp.minimum(jnp.maximum(jnp.concatenate(slot, axis=0).astype(i32), 0), SLOTS - 1)
    back_ref[...] = jnp.concatenate(
        [mine * (SLOTS // 2) + (slot >> 1), ((slot + kept) & 1) * TILE], axis=0
    )


def exchange_kernel(
    cols_hbm, fock_ref, amps_hbm, own, recv, back_ref,
    land, fa, amps, send, cols_ref, vtab, vown, stab, sown,
    gsend, grecv, csend, crecv, tsend, trecv, lsem,
):
    zi = lax.axis_index("pairs")
    vi = lax.axis_index("virt")
    pos = {"x": vi // 8, "y": lax.rem(vi // 2, 4), "z": zi, "c": lax.rem(vi, 2)}
    twin = {**pos, "c": 1 - pos["c"]}

    load_amps = pltpu.make_async_copy(amps_hbm, amps, lsem.at[0])

    barrier = pltpu.get_barrier_semaphore()

    def greet(off, carry):
        pl.semaphore_signal(
            barrier, inc=1, device_id=(zi, lax.rem(vi + off, NTILES)), device_id_type=MESH
        )
        return carry

    for off in range(1, NTILES):
        greet(off, 0)
    for by in (1, 2, 3):
        pl.semaphore_signal(
            barrier, inc=1, device_id=place(moved(pos, "z", by)), device_id_type=MESH
        )
    load_cols = pltpu.make_async_copy(cols_hbm, cols_ref, lsem.at[1])
    load_cols.start()
    load_amps.start()
    load_rows = pltpu.make_async_copy(
        fock_ref, land.at[pos["z"], pos["x"], pos["y"], pos["c"]], lsem.at[2]
    )
    load_rows.start()
    load_rows.wait()
    pl.semaphore_wait(barrier, NTILES - 1 + 3)

    sent = []

    def rows_at(where, full, half):
        at = [slice(None) if axis in full else where[axis] for axis in "zxy"]
        cols = slice(None) if half is None else pl.ds(half * HALF, HALF)
        return land.at[at[0], at[1], at[2], where["c"], :, cols]

    def copy_to(target, number, src, dst, out=gsend, into=grecv):
        return pltpu.make_async_remote_copy(
            src_ref=src, dst_ref=dst, send_sem=out.at[number], recv_sem=into.at[number],
            device_id=place(target), device_id_type=MESH,
        )

    def push(axis, by, number, where, full="", half=None):
        ref = rows_at(where, full, half)
        copy = copy_to(moved(pos, axis, by), number, ref, ref)
        copy.start()
        sent.append(copy)

    def arrived(number, where, full="", half=None):
        ref = rows_at(where, full, half)
        copy_to(twin, number, ref, ref).wait_recv()

    def across(number, where, full="", half=None):
        ref = rows_at(where, full, half)
        copy = copy_to(twin, number, ref, ref, csend, crecv)
        copy.start()
        sent.append(copy)

    def came_across(number, where, full="", half=None):
        ref = rows_at({**where, "c": twin["c"]}, full, half)
        copy_to(twin, number, ref, ref, csend, crecv).wait_recv()

    def far(g):
        return moved(pos, "x", -g)

    def far_first(g):
        arrived(g - 1, far(g), half=0)
        for by in (1, 2, 3):
            push("y", by, 15 + 6 * (g - 1) + by - 1, far(g), half=0)

    def far_second(g):
        for by in (1, 2, 3):
            arrived(15 + 6 * (g - 1) + by - 1, moved(far(g), "y", -by), half=0)
        arrived(32 + g, far(g), "y", half=1)
        for by in (1, 2, 3):
            push("z", by, 18 + 6 * (g - 1) + by - 1, far(g), "y")
        across(8 + 4 * (g - 1), far(g), "y")

    def far_third(g):
        for by in (1, 2, 3):
            there = moved(far(g), "z", -by)
            arrived(18 + 6 * (g - 1) + by - 1, there, "y")
            across(8 + 4 * (g - 1) + by, there, "y")

    def far_last(g):
        for by in range(4):
            came_across(8 + 4 * (g - 1) + by, moved(far(g), "z", -by), "y")

    for by in (1, 2, 3):
        push("z", by, 3 + by - 1, pos, half=0)
        push("y", by, 6 + by - 1, pos, half=1)
    for by in (1, 2, 3):
        push("x", by, by - 1, pos, half=0)
    load_cols.wait()
    write_tables(vi, cols_ref, vtab, vown, back_ref)
    job_table = pltpu.make_async_copy(vtab, stab, lsem.at[1])
    own_table = pltpu.make_async_copy(vown, sown, lsem.at[2])
    job_table.start()
    own_table.start()
    for half, axis, other in ((0, "z", "y"), (1, "y", "z")):
        for by in (1, 2, 3):
            arrived(3 + 3 * half + by - 1, moved(pos, axis, -by), half=half)
        for by in (1, 2, 3):
            push(other, by, 9 + 3 * half + by - 1, pos, axis, half)
        across(4 * half, pos, axis, half)
    for by in (1, 2, 3):
        push("x", by, 32 + by, pos, "y", half=1)
    for g in (1, 2, 3):
        far_first(g)
    for by in (1, 2, 3):
        for half, axis, other in ((0, "z", "y"), (1, "y", "z")):
            there = moved(pos, other, -by)
            arrived(9 + 3 * half + by - 1, there, axis, half)
            across(4 * half + by, there, axis, half)
    far_second(1)
    for by in range(4):
        for half, axis, other in ((0, "z", "y"), (1, "y", "z")):
            came_across(4 * half + by, moved(pos, other, -by), axis, half)
    job_table.wait()
    own_table.wait()
    load_amps.wait()

    def spread(zs, xs, high):
        tile = zs * 8 + xs * 2 + high
        for part in range(4):
            for t in range(LANES):
                got = land[zs, xs, high * 2 + part // 2, part % 2, :, t * 128:(t + 1) * 128]
                fa[t, tile, part * 16:(part + 1) * 16] = got
                fa[LANES + t, tile, part * 16:(part + 1) * 16] = jnp.concatenate(
                    [got[:, TILE:], got[:, :TILE]], axis=1
                )

    low = lax.broadcasted_iota(jnp.int32, (TILE, 128), 1) < TILE

    def tile_row(tile, cols):
        got = [fa[col, tile] for col in cols]
        return jnp.concatenate(
            [jnp.where(low, got[0], got[1]), jnp.where(low, got[2], got[3])], axis=1
        )

    def dressed(tile, slot):
        at = tile * SLOTS + slot
        cols = [stab[k, at] for k in range(KEPT)]
        return lax.dot_general(
            tile_row(tile, cols), amps[stab[KEPT, at]], (((1,), (1,)), ((), ())),
            preferred_element_type=jnp.float32,
        )

    def tile_copy(tile, split):
        return pltpu.make_async_remote_copy(
            src_ref=send.at[tile, split], dst_ref=recv.at[vi, split],
            send_sem=tsend.at[tile * SPLITS + split], recv_sem=trecv.at[vi * SPLITS + split],
            device_id=(zi, tile), device_id_type=MESH,
        )

    def self_copy(split):
        return pltpu.make_async_copy(
            send.at[vi, split], recv.at[vi, split], tsend.at[vi * SPLITS + split]
        )

    def group(g):
        xs = lax.rem(pos["x"] + 4 - g, 4)

        def mirror(step, carry):
            split = step // 8
            at = lax.rem(step, 8)
            turn = lax.rem(at, 4) + 2 * (at // 4) + pos["y"] + 2 * pos["c"] + 3 * split + 1
            zs, high = lax.rem(pos["x"] + turn, 4), lax.rem(at // 4 + pos["c"], 2)
            tile = zs * 8 + xs * 2 + high

            @pl.when(split == 0)
            def _():
                spread(zs, xs, high)

            for s in range(0, PER, 2):
                pair = [dressed(tile, split * PER + s + i).astype(jnp.bfloat16) for i in (0, 1)]
                send[tile, split, s // 2] = jnp.concatenate(pair, axis=1)

            @pl.when(tile != vi)
            def _():
                tile_copy(tile, split).start()

            @pl.when(tile == vi)
            def _():
                self_copy(split).start()

            return carry

        lax.fori_loop(0, 8 * SPLITS, mirror, 0)

    group(0)
    far_third(1)
    far_second(2)
    far_last(1)
    group(1)
    far_third(2)
    far_second(3)
    far_last(2)
    group(2)
    far_third(3)
    far_last(3)
    group(3)

    def own_row(row, carry):
        cols = [sown[k, row] for k in range(KEPT)]
        weights = jnp.concatenate(
            [tile_row(sown[KEPT + k, row], cols) for k in range(KEPT)], axis=0
        )
        own[row] = lax.dot_general(
            amps[row], weights, (((1,), (1,)), ((), ())), preferred_element_type=jnp.float32
        )
        return carry

    lax.fori_loop(0, ROWS, own_row, 0)
    for copy in sent:
        copy.wait_send()

    def finish(step, carry):
        g, split, at = step // (8 * SPLITS), lax.rem(step // 8, SPLITS), lax.rem(step, 8)
        tile = (at // 2) * 8 + lax.rem(pos["x"] + 4 - g, 4) * 2 + lax.rem(at, 2)
        peer = lax.rem(pos["y"] + g, 4) * 8 + at

        @pl.when(tile != vi)
        def _():
            tile_copy(tile, split).wait_send()

        @pl.when(tile == vi)
        def _():
            self_copy(split).wait()

        @pl.when(peer != vi)
        def _():
            pltpu.make_async_remote_copy(
                src_ref=send.at[peer, split], dst_ref=recv.at[peer, split],
                send_sem=tsend.at[peer * SPLITS + split], recv_sem=trecv.at[peer * SPLITS + split],
                device_id=(zi, peer), device_id_type=MESH,
            ).wait_recv()

        return carry

    lax.fori_loop(0, NTILES * SPLITS, finish, 0)


def combine_kernel(back_ref, own, recv, out_hbm, out, out_sem):
    def store(number):
        part = pl.ds(pl.multiple_of(number * CHUNK, CHUNK), CHUNK)
        return pltpu.make_async_copy(out.at[part], out_hbm.at[part], out_sem.at[number])

    low = lax.broadcasted_iota(jnp.int32, (TILE, 128), 1) < TILE

    def part(number, carry):
        def some_rows(some, carry):
            for r in range(4):
                row = number * CHUNK + some * 4 + r
                for h in range(2):
                    lanes = pl.ds(h * 128, 128)
                    left, right = [recv[back_ref[2 * h + i, row]] for i in range(2)]
                    turns = [back_ref[KEPT + 2 * h + i, row] for i in range(2)]
                    kept = jnp.where(low, left, right)
                    other = jnp.where(low, right, left)
                    other = jnp.concatenate([other[:, TILE:], other[:, :TILE]], axis=1)
                    stay = jnp.where(low, turns[0], turns[1]) == 0
                    out[row, :, lanes] = own[row, :, lanes] + jnp.where(
                        stay, kept.astype(jnp.float32), other.astype(jnp.float32)
                    )
            return carry

        lax.fori_loop(0, CHUNK // 4, some_rows, 0)
        store(number).start()
        return carry

    lax.fori_loop(0, ROWS // CHUNK, part, 0)
    for number in range(ROWS // CHUNK):
        store(number).wait()


def per_device(amps, fock, cols):
    vmem = pl.BlockSpec(memory_space=pltpu.VMEM)
    smem = pl.BlockSpec(memory_space=pltpu.SMEM)
    anywhere = pl.BlockSpec(memory_space=pl.ANY)
    own, received, back = pl.pallas_call(
        exchange_kernel,
        out_shape=(
            pltpu.VMEM((ROWS, TILE, KEPT * TILE), jnp.float32),
            pltpu.VMEM((NTILES, SPLITS, PER // 2, TILE, 2 * TILE), jnp.bfloat16),
            jax.ShapeDtypeStruct((2 * KEPT, ROWS), jnp.int32),
        ),
        in_specs=[anywhere, anywhere, anywhere],
        out_specs=(vmem, vmem, vmem),
        scratch_shapes=[
            pltpu.VMEM((4, 4, 4, 2, 16, 2048), jnp.bfloat16),
            pltpu.VMEM((2 * LANES, NTILES, TILE, 128), jnp.bfloat16),
            pltpu.VMEM((ROWS, TILE, KEPT * TILE), jnp.bfloat16),
            pltpu.VMEM((NTILES, SPLITS, PER // 2, TILE, 2 * TILE), jnp.bfloat16),
            pltpu.VMEM((NTILES, KEPT, ROWS), jnp.int32),
            pltpu.VMEM((8, NTILES * SLOTS), jnp.int32),
            pltpu.VMEM((8, ROWS), jnp.int32),
            pltpu.SMEM((8, NTILES * SLOTS), jnp.int32),
            pltpu.SMEM((8, ROWS), jnp.int32),
            pltpu.SemaphoreType.DMA((36,)),
            pltpu.SemaphoreType.DMA((36,)),
            pltpu.SemaphoreType.DMA((20,)),
            pltpu.SemaphoreType.DMA((20,)),
            pltpu.SemaphoreType.DMA((NTILES * SPLITS,)),
            pltpu.SemaphoreType.DMA((NTILES * SPLITS,)),
            pltpu.SemaphoreType.DMA((3,)),
        ],
        compiler_params=pltpu.CompilerParams(
            collective_id=0, has_side_effects=True, vmem_limit_bytes=42 * 2**20
        ),
    )(cols.transpose(0, 2, 1), fock, amps.reshape(ROWS, TILE, KEPT * TILE))
    out = pl.pallas_call(
        combine_kernel,
        out_shape=jax.ShapeDtypeStruct((ROWS, TILE, KEPT * TILE), jnp.float32),
        in_specs=[smem, vmem, vmem],
        out_specs=anywhere,
        scratch_shapes=[
            pltpu.VMEM((ROWS, TILE, KEPT * TILE), jnp.float32),
            pltpu.SemaphoreType.DMA((ROWS // CHUNK,)),
        ],
        compiler_params=pltpu.CompilerParams(vmem_limit_bytes=12 * 2**20),
    )(back, own, received.reshape(NTILES * SLOTS // 2, TILE, 2 * TILE))
    return out[None]


def solution(mesh):
    in_specs = (P("virt", "pairs", None, None), P(("pairs", "virt"), None), P(None, "pairs", None))
    out_specs = P("virt", "pairs", None, None)
    return jax.shard_map(
        per_device, mesh=mesh, in_specs=in_specs, out_specs=out_specs, check_vma=False
    )
```

```python
import functools

import jax
import jax.numpy as jnp
from jax import lax
from jax.experimental import pallas as pl
from jax.experimental.pallas import tpu as pltpu
from jax.sharding import PartitionSpec as P

MESH = pl.DeviceIdType.MESH
TILE = 64
KEPT = 4
ROWS = 128
NTILES = 32
NSIDE = 4
SPLITS = 4
SLOTS = 32
PER = SLOTS // SPLITS
LANES = 16
CHUNK = 8
HALF = 1024


def place(pos):
    return (pos["z"], pos["x"] * 8 + pos["y"] * 2 + pos["c"])


def moved(pos, axis, by):
    new = dict(pos)
    new[axis] = lax.rem(pos[axis] + by + 4, 4)
    return new


def write_tables(me, cols_ref, vtab, vown, back_ref):
    f32, bf16, i32 = jnp.float32, jnp.bfloat16, jnp.int32
    mine = cols_ref[me]
    kept = lax.broadcasted_iota(i32, (KEPT, ROWS), 0)
    lane = lax.broadcasted_iota(i32, (KEPT, ROWS), 1)
    mine = jnp.minimum(jnp.maximum(mine, 0), NTILES - 1)
    spot = ((mine + kept) & 1) * LANES + (mine >> 1)
    vown[...] = jnp.concatenate([spot, mine], axis=0)
    first = lax.broadcasted_iota(i32, (ROWS, ROWS), 0)
    second = lax.broadcasted_iota(i32, (ROWS, ROWS), 1)
    upper = (first <= second).astype(f32).astype(bf16)
    flip = (first + second == ROWS - 1).astype(f32).astype(bf16)
    about = jnp.concatenate([spot, lane], axis=0).astype(f32).astype(bf16)
    about = jnp.dot(about, flip, preferred_element_type=f32).astype(bf16)
    named = jnp.sum((cols_ref[...] == me).astype(f32), axis=1)
    upto = jnp.dot(named.astype(bf16), upper, preferred_element_type=f32)
    rank = jnp.where(named > 0, upto, 0.0)
    slots = lax.broadcasted_iota(i32, (SLOTS, ROWS), 0).astype(f32) + 1.0
    entry = lax.broadcasted_iota(i32, (8, 8 * SLOTS), 0)
    largest = jnp.where(entry < KEPT, 2 * LANES - 1, ROWS - 1)
    for peer in range(0, NTILES, 8):
        hot = [
            (jnp.broadcast_to(rank[p:p + 1], (SLOTS, ROWS)) == slots).astype(f32).astype(bf16)
            for p in range(peer, peer + 8)
        ]
        got = lax.dot_general(
            about, jnp.concatenate(hot, axis=0), (((1,), (1,)), ((), ())),
            preferred_element_type=f32,
        )
        got = jnp.minimum(jnp.maximum(got.astype(i32), 0), largest)
        vtab[:, peer * SLOTS:(peer + 8) * SLOTS] = got
    number = lax.broadcasted_iota(i32, (NTILES, ROWS), 0)
    at = [jnp.broadcast_to(mine[k:k + 1], (NTILES, ROWS)) == number for k in range(KEPT)]
    count = sum(hit.astype(f32) for hit in at)
    before = jnp.dot(count.astype(bf16), upper, preferred_element_type=f32) - count
    slot = [jnp.sum(jnp.where(hit, before, 0.0), axis=0, keepdims=True) for hit in at]
    slot = jnp.minimum(jnp.maximum(jnp.concatenate(slot, axis=0).astype(i32), 0), SLOTS - 1)
    back_ref[...] = jnp.concatenate(
        [mine * (SLOTS // 2) + (slot >> 1), ((slot + kept) & 1) * TILE], axis=0
    )


def exchange_kernel(
    cols_hbm, fock_ref, amps_hbm, own, recv, back_ref,
    land, fa, amps, send, cols_ref, vtab, vown, stab, sown,
    gsend, grecv, csend, crecv, tsend, trecv, lsem,
):
    zi = lax.axis_index("pairs")
    vi = lax.axis_index("virt")
    pos = {"x": vi // 8, "y": lax.rem(vi // 2, 4), "z": zi, "c": lax.rem(vi, 2)}
    twin = {**pos, "c": 1 - pos["c"]}

    load_amps = pltpu.make_async_copy(amps_hbm, amps, lsem.at[0])

    barrier = pltpu.get_barrier_semaphore()

    def greet(off, carry):
        pl.semaphore_signal(
            barrier, inc=1, device_id=(zi, lax.rem(vi + off, NTILES)), device_id_type=MESH
        )
        return carry

    for off in range(1, NTILES):
        greet(off, 0)
    for by in (1, 2, 3):
        pl.semaphore_signal(
            barrier, inc=1, device_id=place(moved(pos, "z", by)), device_id_type=MESH
        )
    load_cols = pltpu.make_async_copy(cols_hbm, cols_ref, lsem.at[1])
    load_cols.start()
    load_amps.start()
    load_rows = pltpu.make_async_copy(
        fock_ref, land.at[pos["z"], pos["x"], pos["y"], pos["c"]], lsem.at[2]
    )
    load_rows.start()
    load_rows.wait()
    pl.semaphore_wait(barrier, NTILES - 1 + 3)

    sent = []

    def rows_at(where, full, half):
        at = [slice(None) if axis in full else where[axis] for axis in "zxy"]
        cols = slice(None) if half is None else pl.ds(half * HALF, HALF)
        return land.at[at[0], at[1], at[2], where["c"], :, cols]

    def copy_to(target, number, src, dst, out=gsend, into=grecv):
        return pltpu.make_async_remote_copy(
            src_ref=src, dst_ref=dst, send_sem=out.at[number], recv_sem=into.at[number],
            device_id=place(target), device_id_type=MESH,
        )

    def push(axis, by, number, where, full="", half=None):
        ref = rows_at(where, full, half)
        copy = copy_to(moved(pos, axis, by), number, ref, ref)
        copy.start()
        sent.append(copy)

    def arrived(number, where, full="", half=None):
        ref = rows_at(where, full, half)
        copy_to(twin, number, ref, ref).wait_recv()

    def across(number, where, full="", half=None):
        ref = rows_at(where, full, half)
        copy = copy_to(twin, number, ref, ref, csend, crecv)
        copy.start()
        sent.append(copy)

    def came_across(number, where, full="", half=None):
        ref = rows_at({**where, "c": twin["c"]}, full, half)
        copy_to(twin, number, ref, ref, csend, crecv).wait_recv()

    def far(g):
        return moved(pos, "x", -g)

    def far_first(g):
        arrived(g - 1, far(g), half=0)
        for by in (1, 2, 3):
            push("y", by, 15 + 6 * (g - 1) + by - 1, far(g), half=0)

    def far_second(g):
        for by in (1, 2, 3):
            arrived(15 + 6 * (g - 1) + by - 1, moved(far(g), "y", -by), half=0)
        arrived(32 + g, far(g), "y", half=1)
        for by in (1, 2, 3):
            push("z", by, 18 + 6 * (g - 1) + by - 1, far(g), "y")
        across(8 + 4 * (g - 1), far(g), "y")

    def far_third(g):
        for by in (1, 2, 3):
            there = moved(far(g), "z", -by)
            arrived(18 + 6 * (g - 1) + by - 1, there, "y")
            across(8 + 4 * (g - 1) + by, there, "y")

    def far_last(g):
        for by in range(4):
            came_across(8 + 4 * (g - 1) + by, moved(far(g), "z", -by), "y")

    for by in (1, 2, 3):
        push("z", by, 3 + by - 1, pos, half=0)
        push("y", by, 6 + by - 1, pos, half=1)
    for by in (1, 2, 3):
        push("x", by, by - 1, pos, half=0)
    load_cols.wait()
    write_tables(vi, cols_ref, vtab, vown, back_ref)
    job_table = pltpu.make_async_copy(vtab, stab, lsem.at[1])
    own_table = pltpu.make_async_copy(vown, sown, lsem.at[2])
    job_table.start()
    own_table.start()
    for half, axis, other in ((0, "z", "y"), (1, "y", "z")):
        for by in (1, 2, 3):
            arrived(3 + 3 * half + by - 1, moved(pos, axis, -by), half=half)
        for by in (1, 2, 3):
            push(other, by, 9 + 3 * half + by - 1, pos, axis, half)
        across(4 * half, pos, axis, half)
    for by in (1, 2, 3):
        push("x", by, 32 + by, pos, "y", half=1)
    for g in (1, 2, 3):
        far_first(g)
    for by in (1, 2, 3):
        for half, axis, other in ((0, "z", "y"), (1, "y", "z")):
            there = moved(pos, other, -by)
            arrived(9 + 3 * half + by - 1, there, axis, half)
            across(4 * half + by, there, axis, half)
    far_second(1)
    for by in range(4):
        for half, axis, other in ((0, "z", "y"), (1, "y", "z")):
            came_across(4 * half + by, moved(pos, other, -by), axis, half)
    job_table.wait()
    own_table.wait()
    load_amps.wait()

    def spread(zs, xs, high):
        tile = zs * 8 + xs * 2 + high
        for part in range(4):
            for t in range(LANES):
                got = land[zs, xs, high * 2 + part // 2, part % 2, :, t * 128:(t + 1) * 128]
                fa[t, tile, part * 16:(part + 1) * 16] = got
                fa[LANES + t, tile, part * 16:(part + 1) * 16] = jnp.concatenate(
                    [got[:, TILE:], got[:, :TILE]], axis=1
                )

    low = lax.broadcasted_iota(jnp.int32, (TILE, 128), 1) < TILE

    def tile_row(tile, cols):
        got = [fa[col, tile] for col in cols]
        return jnp.concatenate(
            [jnp.where(low, got[0], got[1]), jnp.where(low, got[2], got[3])], axis=1
        )

    def dressed(tile, slot):
        at = tile * SLOTS + slot
        cols = [stab[k, at] for k in range(KEPT)]
        return lax.dot_general(
            tile_row(tile, cols), amps[stab[KEPT, at]], (((1,), (1,)), ((), ())),
            preferred_element_type=jnp.float32,
        )

    def tile_copy(tile, split):
        return pltpu.make_async_remote_copy(
            src_ref=send.at[tile, split], dst_ref=recv.at[vi, split],
            send_sem=tsend.at[tile * SPLITS + split], recv_sem=trecv.at[vi * SPLITS + split],
            device_id=(zi, tile), device_id_type=MESH,
        )

    def self_copy(split):
        return pltpu.make_async_copy(
            send.at[vi, split], recv.at[vi, split], tsend.at[vi * SPLITS + split]
        )

    def group(g):
        xs = lax.rem(pos["x"] + 4 - g, 4)

        def mirror(step, carry):
            split = step // 8
            at = lax.rem(step, 8)
            turn = lax.rem(at, 4) + 2 * (at // 4) + pos["y"] + 2 * pos["c"] + 3 * split + 1
            zs, high = lax.rem(pos["x"] + turn, 4), lax.rem(at // 4 + pos["c"], 2)
            tile = zs * 8 + xs * 2 + high

            @pl.when(split == 0)
            def _():
                spread(zs, xs, high)

            for s in range(0, PER, 2):
                pair = [dressed(tile, split * PER + s + i).astype(jnp.bfloat16) for i in (0, 1)]
                send[tile, split, s // 2] = jnp.concatenate(pair, axis=1)

            @pl.when(tile != vi)
            def _():
                tile_copy(tile, split).start()

            @pl.when(tile == vi)
            def _():
                self_copy(split).start()

            return carry

        lax.fori_loop(0, 8 * SPLITS, mirror, 0)

    group(0)
    far_third(1)
    far_second(2)
    far_last(1)
    group(1)
    far_third(2)
    far_second(3)
    far_last(2)
    group(2)
    far_third(3)
    far_last(3)
    group(3)

    def own_row(row, carry):
        cols = [sown[k, row] for k in range(KEPT)]
        weights = jnp.concatenate(
            [tile_row(sown[KEPT + k, row], cols) for k in range(KEPT)], axis=0
        )
        own[row] = lax.dot_general(
            amps[row], weights, (((1,), (1,)), ((), ())), preferred_element_type=jnp.float32
        )
        return carry

    lax.fori_loop(0, ROWS, own_row, 0)
    for copy in sent:
        copy.wait_send()

    def finish(step, carry):
        g, split, at = step // (8 * SPLITS), lax.rem(step // 8, SPLITS), lax.rem(step, 8)
        tile = (at // 2) * 8 + lax.rem(pos["x"] + 4 - g, 4) * 2 + lax.rem(at, 2)
        peer = lax.rem(pos["y"] + g, 4) * 8 + at

        @pl.when(tile != vi)
        def _():
            tile_copy(tile, split).wait_send()

        @pl.when(tile == vi)
        def _():
            self_copy(split).wait()

        @pl.when(peer != vi)
        def _():
            pltpu.make_async_remote_copy(
                src_ref=send.at[peer, split], dst_ref=recv.at[peer, split],
                send_sem=tsend.at[peer * SPLITS + split], recv_sem=trecv.at[peer * SPLITS + split],
                device_id=(zi, peer), device_id_type=MESH,
            ).wait_recv()

        return carry

    lax.fori_loop(0, NTILES * SPLITS, finish, 0)


def combine_kernel(back_ref, own, recv, out_hbm, out, out_sem):
    def store(number):
        part = pl.ds(pl.multiple_of(number * CHUNK, CHUNK), CHUNK)
        return pltpu.make_async_copy(out.at[part], out_hbm.at[part], out_sem.at[number])

    low = lax.broadcasted_iota(jnp.int32, (TILE, 128), 1) < TILE

    def part(number, carry):
        def some_rows(some, carry):
            for r in range(8):
                row = number * CHUNK + some * 8 + r
                for h in range(2):
                    lanes = pl.ds(h * 128, 128)
                    left, right = [recv[back_ref[2 * h + i, row]] for i in range(2)]
                    turns = [back_ref[KEPT + 2 * h + i, row] for i in range(2)]
                    kept = jnp.where(low, left, right)
                    other = jnp.where(low, right, left)
                    other = jnp.concatenate([other[:, TILE:], other[:, :TILE]], axis=1)
                    stay = jnp.where(low, turns[0], turns[1]) == 0
                    out[row, :, lanes] = own[row, :, lanes] + jnp.where(
                        stay, kept.astype(jnp.float32), other.astype(jnp.float32)
                    )
            return carry

        lax.fori_loop(0, CHUNK // 8, some_rows, 0)
        store(number).start()
        return carry

    lax.fori_loop(0, ROWS // CHUNK, part, 0)
    for number in range(ROWS // CHUNK):
        store(number).wait()


def per_device(amps, fock, cols):
    vmem = pl.BlockSpec(memory_space=pltpu.VMEM)
    smem = pl.BlockSpec(memory_space=pltpu.SMEM)
    anywhere = pl.BlockSpec(memory_space=pl.ANY)
    own, received, back = pl.pallas_call(
        exchange_kernel,
        out_shape=(
            pltpu.VMEM((ROWS, TILE, KEPT * TILE), jnp.float32),
            pltpu.VMEM((NTILES, SPLITS, PER // 2, TILE, 2 * TILE), jnp.bfloat16),
            jax.ShapeDtypeStruct((2 * KEPT, ROWS), jnp.int32),
        ),
        in_specs=[anywhere, anywhere, anywhere],
        out_specs=(vmem, vmem, vmem),
        scratch_shapes=[
            pltpu.VMEM((4, 4, 4, 2, 16, 2048), jnp.bfloat16),
            pltpu.VMEM((2 * LANES, NTILES, TILE, 128), jnp.bfloat16),
            pltpu.VMEM((ROWS, TILE, KEPT * TILE), jnp.bfloat16),
            pltpu.VMEM((NTILES, SPLITS, PER // 2, TILE, 2 * TILE), jnp.bfloat16),
            pltpu.VMEM((NTILES, KEPT, ROWS), jnp.int32),
            pltpu.VMEM((8, NTILES * SLOTS), jnp.int32),
            pltpu.VMEM((8, ROWS), jnp.int32),
            pltpu.SMEM((8, NTILES * SLOTS), jnp.int32),
            pltpu.SMEM((8, ROWS), jnp.int32),
            pltpu.SemaphoreType.DMA((36,)),
            pltpu.SemaphoreType.DMA((36,)),
            pltpu.SemaphoreType.DMA((20,)),
            pltpu.SemaphoreType.DMA((20,)),
            pltpu.SemaphoreType.DMA((NTILES * SPLITS,)),
            pltpu.SemaphoreType.DMA((NTILES * SPLITS,)),
            pltpu.SemaphoreType.DMA((3,)),
        ],
        compiler_params=pltpu.CompilerParams(
            collective_id=0, has_side_effects=True, vmem_limit_bytes=42 * 2**20
        ),
    )(cols.transpose(0, 2, 1), fock, amps.reshape(ROWS, TILE, KEPT * TILE))
    out = pl.pallas_call(
        combine_kernel,
        out_shape=jax.ShapeDtypeStruct((ROWS, TILE, KEPT * TILE), jnp.float32),
        in_specs=[smem, vmem, vmem],
        out_specs=anywhere,
        scratch_shapes=[
            pltpu.VMEM((ROWS, TILE, KEPT * TILE), jnp.float32),
            pltpu.SemaphoreType.DMA((ROWS // CHUNK,)),
        ],
        compiler_params=pltpu.CompilerParams(vmem_limit_bytes=12 * 2**20),
    )(back, own, received.reshape(NTILES * SLOTS // 2, TILE, 2 * TILE))
    return out[None]


def solution(mesh):
    in_specs = (P("virt", "pairs", None, None), P(("pairs", "virt"), None), P(None, "pairs", None))
    out_specs = P("virt", "pairs", None, None)
    return jax.shard_map(
        per_device, mesh=mesh, in_specs=in_specs, out_specs=out_specs, check_vma=False
    )
```
